128 devices in a mesh: row: 16 (over x, z), col: 8 (over y, core).
Axes of the slice: x: 4, y: 4, z: 4, core: 2. Of those that a mesh axis runs over, the one named last changes fastest.
Arguments:
- trailing: float32 [20480, 20480], P('row', 'col'), may hold values from -28 to 28
- panel_block: float32 [20480, 256], P('row', 'col'), as said below
Outputs:
- updated: float32 [20480, 20480], P('row', 'col')
The draws below stay inside these ranges and needn't reach their ends.
Inputs may be any that keep to these rules, and one draw needn't show every extreme that they name: `panel_block`: entry (j, j) of each of the first 256 rows is 2 * sqrt(20480) plus a term within 7 of zero; every other entry lies within 7 of zero.
All inputs are finite; a program needn't handle non-finite values.
Results may differ from the reference program's by a relative error of at most 0.000064.
Values sent between devices are 32-bit elements; how exact they have to be, the bound alone decides.
No kernel may reach another device: no remote copies, remote signals or barrier semaphores. Data moves between devices by JAX's collectives and lax.ppermute only.
A program may use at most 128 MiB of HBM per device.

```python
import math
import jax
import jax.numpy as jnp
from jax import lax

M = 20480
B = 256


def draw_trailing(key, part):
    key = jax.random.fold_in(key, 11)
    noise_key = jax.random.fold_in(key, 0)
    raw = jnp.clip(jax.random.normal(noise_key, (M, M), jnp.float32), -6.0, 6.0)
    return (0.5 * (raw + raw.T)).astype(jnp.float32)


def draw_panel_block(key, part):
    key = jax.random.fold_in(key, 23)
    noise_key = jax.random.fold_in(key, 0)
    raw = jnp.clip(jax.random.normal(noise_key, (M, B), jnp.float32), -6.0, 6.0)
    boost = 2.0 * math.sqrt(M) * jnp.eye(M, B, dtype=jnp.float32)
    return (raw + boost).astype(jnp.float32)


def setup_inputs(seed: int = 0) -> dict:
    key_list = jax.random.split(jax.random.key(seed), 3)
    trailing = draw_trailing(jax.random.fold_in(key_list[2], 71), 0)
    panel_block = draw_panel_block(jax.random.fold_in(key_list[2], 71), 0)
    return {"trailing": trailing, "panel_block": panel_block}


def reference(trailing, panel_block):
    highest = lax.Precision.HIGHEST
    panel_gram = jnp.dot(panel_block.T, panel_block, precision=highest)
    factor = jnp.linalg.cholesky(panel_gram)
    orthonormal = jax.scipy.linalg.solve_triangular(factor, panel_block.T, lower=True).T
    reflect = orthonormal + jnp.eye(M, B, dtype=jnp.float32)
    coupling = jnp.linalg.inv(reflect[:B]).T
    products = jnp.dot(jnp.dot(trailing, reflect, precision=highest), coupling, precision=highest)
    cross_term = jnp.dot(reflect.T, products, precision=highest)
    adjust = products - 0.5 * jnp.dot(reflect, jnp.dot(coupling.T, cross_term, precision=highest), precision=highest)
    return trailing - jnp.dot(reflect, adjust.T, precision=highest) - jnp.dot(adjust, reflect.T, precision=highest)
```

```python
import jax
import jax.numpy as jnp
from jax import lax
from jax.experimental import pallas as pl
from jax.experimental.pallas import tpu as pltpu
from jax.sharding import PartitionSpec as P

W = 256
H = 128
BOTH = ("row", "col")
HIGHEST = lax.Precision.HIGHEST
HIGH = lax.Precision.HIGH


def lane(x, l):
    if x.shape[0] == 1:
        return lane(jnp.broadcast_to(x, (8, H)), l)[0:1]
    return jnp.take_along_axis(x, jnp.full(x.shape, l, jnp.int32), axis=1, mode="promise_in_bounds")


def factor_kernel(gram_ref, top_ref, lt_ref, tt_ref, gw, vr, lt):
    ri = lax.broadcasted_iota(jnp.int32, (W, W), 0)
    ci = lax.broadcasted_iota(jnp.int32, (W, W), 1)
    g = gram_ref[...]
    scale = 1.0 / jnp.max(jnp.where(ri == ci, g, 0.0), keepdims=True)
    root = jnp.sqrt(scale)
    t = top_ref[...] * root
    g = g * scale
    for h in range(2):
        gw[h] = g[:, h * H : (h + 1) * H]
        vr[h] = t[:, h * H : (h + 1) * H]
    li = lax.broadcasted_iota(jnp.int32, (1, H), 1)

    def chol_step(j, h, row0):
        l = j - h * H
        rows = [gw[k, pl.ds(j, 1), :] for k in range(2)]
        d = lane(rows[h], l)
        rs = lax.rsqrt(d)
        rs = rs * (1.5 - 0.5 * d * rs * rs)
        inv = rs * rs
        mod = [r * inv for r in rows]
        mod[h] = jnp.where(li == l, 1.0 + inv, mod[h])
        col = lane(gw[h, row0:, :], l)
        for k in range(2):
            gw[k, row0:, :] = gw[k, row0:, :] - col * mod[k]
        scaled = [r * rs for r in rows]
        for k in range(2):
            lt[k, pl.ds(j, 1), :] = jnp.where(li + k * H >= j, scaled[k], 0.0)
        return (rs, scaled[0], scaled[1])

    def jordan_step(j, h, carry):
        rs, s0, s1 = carry
        l = j - h * H
        rows = [vr[0, pl.ds(j, 1), :] + s0, vr[1, pl.ds(j, 1), :] + s1]
        q = 1.0 / lane(rows[h], l)
        here = li == l
        norm = [r * q for r in rows]
        mod = list(norm)
        mod[h] = jnp.where(here, 1.0 + rs * q, norm[h])
        norm[h] = jnp.where(here, rs * q, norm[h])
        col = lane(vr[h], l)
        for k in range(2):
            vr[k] = vr[k] - col * mod[k]
        for k in range(2):
            vr[k, pl.ds(j, 1), :] = norm[k]

    seg = 64
    carry = chol_step(0, 0, 0)
    for s in range(W // seg):
        h = s * seg // H
        start = s * seg

        def body(j, carry, h=h, start=start):
            new = chol_step(j, h, start)
            jordan_step(j - 1, h, carry)
            return new

        first = start
        if start % H == 0:
            if s > 0:
                new = chol_step(start, h, start)
                jordan_step(start - 1, h - 1, carry)
                carry = new
            first += 1
        carry = lax.fori_loop(first, start + seg, body, carry)
    jordan_step(W - 1, 1, carry)
    unroot = 1.0 / root
    for k in range(2):
        lt_ref[:, k * H : (k + 1) * H] = lt[k] * unroot
        tt_ref[:, k * H : (k + 1) * H] = vr[k] * scale


def factor(gram, top):
    vmem = pl.BlockSpec(memory_space=pltpu.VMEM)
    return pl.pallas_call(
        factor_kernel,
        out_shape=[jax.ShapeDtypeStruct((W, W), jnp.float32)] * 2,
        in_specs=[vmem] * 2,
        out_specs=[vmem] * 2,
        scratch_shapes=[pltpu.VMEM((2, W, H), jnp.float32)] * 3,
        cost_estimate=pl.CostEstimate(flops=2 * W**3, bytes_accessed=16 * W * W, transcendentals=0),
    )(gram, top)


def to_tiles(x):
    rows, cols = x.shape
    return x.reshape(rows // 8, 8, cols // H, H).transpose(0, 2, 1, 3).reshape(rows * cols // (8 * H), 8, H)


def from_tiles(x, rows, cols):
    return x.reshape(rows // 8, cols // H, 8, H).transpose(0, 2, 1, 3).reshape(rows, cols)


def sum_all(x, axes, parts):
    pieces = x.reshape((parts, -1) + x.shape[1:])
    mine = jnp.sum(lax.all_to_all(pieces, axes, 0, 0, tiled=True), axis=0)
    full = lax.all_to_all(jnp.broadcast_to(mine[None], (parts,) + mine.shape), axes, 0, 0, tiled=True)
    return full.reshape(x.shape)


def shards(trailing, panel_block):
    r = lax.axis_index("row")
    c = lax.axis_index("col")
    nr = lax.axis_size("row")
    nc = lax.axis_size("col")
    ratio = nr // nc
    perm = [(i * nc + j, ((i % ratio) * nc + j) * nc + i // ratio) for i in range(nr) for j in range(nc)]
    rows = panel_block.shape[0]
    part = rows // nc
    panel_t = panel_block.T
    slab = lax.all_to_all(panel_block, "col", 0, 1, tiled=True)
    local_gram = jnp.dot(slab.T, slab, precision=HIGHEST)
    full = jnp.zeros((rows, W), jnp.float32)
    placed = lax.dynamic_update_slice(full, slab, (c * part, 0))[:W]
    placed = jnp.where(r == 0, placed, jnp.zeros_like(placed))
    both = to_tiles(jnp.concatenate([local_gram, placed], axis=1))
    both = from_tiles(sum_all(both, BOTH, nr * nc), W, 2 * W)
    panel_rows = lax.all_gather(panel_t, "col", axis=0, tiled=True)
    moved = lax.ppermute(panel_t, BOTH, perm)
    panel_cols = lax.all_gather(moved, "row", axis=0, tiled=True).reshape(ratio, W, rows)
    factor_t, coupling_t = factor(both[:, :W], both[:, W:])
    lower = factor_t.T
    add_rows = jnp.where(r == 0, lower, jnp.zeros_like(lower))
    add_cols = jnp.where(c == 0, lower, jnp.zeros_like(lower))
    reflect_rows = panel_rows + jnp.pad(add_rows, ((0, 0), (0, rows - W)))
    reflect_cols = jnp.concatenate([panel_cols[i] for i in range(ratio)], axis=1)
    reflect_cols = reflect_cols + jnp.pad(add_cols, ((0, 0), (0, ratio * rows - W)))
    partial = lax.dot_general(trailing, reflect_cols, (((1,), (1,)), ((), ())), precision=HIGH)
    inner = jnp.dot(reflect_rows, partial, precision=HIGH)
    pieces = lax.all_to_all(partial.reshape(nc, part, W), "col", 0, 0, tiled=True)
    mine = jnp.sum(pieces, axis=0)
    mine = lax.dot_general(mine, coupling_t, (((1,), (1,)), ((), ())), precision=HIGHEST)
    moved = lax.ppermute(mine, BOTH, perm)
    weight_cols = lax.all_gather(moved, "row", axis=0, tiled=True)
    weight_rows = lax.all_gather(mine, "col", axis=0, tiled=True)
    inner = sum_all(inner, BOTH, nr * nc)
    inner = jnp.dot(coupling_t, inner, precision=HIGHEST)
    inner = lax.dot_general(inner, coupling_t, (((1,), (1,)), ((), ())), precision=HIGHEST) * 0.5
    weight_cols = weight_cols - lax.dot_general(reflect_cols, inner, (((0,), (0,)), ((), ())), precision=HIGH)
    weight_rows = weight_rows - lax.dot_general(reflect_rows, inner, (((0,), (0,)), ((), ())), precision=HIGH)
    first = lax.dot_general(reflect_rows, weight_cols, (((0,), (1,)), ((), ())), precision=HIGH)
    second = jnp.dot(weight_rows, reflect_cols, precision=HIGH)
    return trailing - first - second


def solution(mesh):
    return jax.shard_map(shards, mesh=mesh, in_specs=(P("row", "col"), P("row", "col")), out_specs=P("row", "col"), check_vma=False)
```

```python
import jax
import jax.numpy as jnp
from jax import lax
from jax.experimental import pallas as pl
from jax.experimental.pallas import tpu as pltpu
from jax.sharding import PartitionSpec as P

W = 256
H = 128
BOTH = ("row", "col")
HIGHEST = lax.Precision.HIGHEST
HIGH = lax.Precision.HIGH


def lane(x, l):
    if x.shape[0] == 1:
        return lane(jnp.broadcast_to(x, (8, H)), l)[0:1]
    return jnp.take_along_axis(x, jnp.full(x.shape, l, jnp.int32), axis=1, mode="promise_in_bounds")


def factor_kernel(gram_ref, top_ref, lt_ref, tt_ref, gw, vr, lt):
    ri = lax.broadcasted_iota(jnp.int32, (W, W), 0)
    ci = lax.broadcasted_iota(jnp.int32, (W, W), 1)
    g = gram_ref[...]
    scale = 1.0 / jnp.max(jnp.where(ri == ci, g, 0.0), keepdims=True)
    root = jnp.sqrt(scale)
    t = top_ref[...] * root
    g = g * scale
    for h in range(2):
        gw[h] = g[:, h * H : (h + 1) * H]
        vr[h] = t[:, h * H : (h + 1) * H]
    li = lax.broadcasted_iota(jnp.int32, (1, H), 1)

    def chol_step(j, h, row0):
        l = j - h * H
        rows = [gw[k, pl.ds(j, 1), :] for k in range(2)]
        d = lane(rows[h], l)
        rs = lax.rsqrt(d)
        rs = rs * (1.5 - 0.5 * d * rs * rs)
        inv = rs * rs
        mod = [r * inv for r in rows]
        mod[h] = jnp.where(li == l, 1.0 + inv, mod[h])
        col = lane(gw[h, row0:, :], l)
        for k in range(2):
            gw[k, row0:, :] = gw[k, row0:, :] - col * mod[k]
        scaled = [r * rs for r in rows]
        for k in range(2):
            lt[k, pl.ds(j, 1), :] = jnp.where(li + k * H >= j, scaled[k], 0.0)
        return (rs, scaled[0], scaled[1])

    def jordan_step(j, h, carry):
        rs, s0, s1 = carry
        l = j - h * H
        rows = [vr[0, pl.ds(j, 1), :] + s0, vr[1, pl.ds(j, 1), :] + s1]
        q = 1.0 / lane(rows[h], l)
        here = li == l
        norm = [r * q for r in rows]
        mod = list(norm)
        mod[h] = jnp.where(here, 1.0 + rs * q, norm[h])
        norm[h] = jnp.where(here, rs * q, norm[h])
        col = lane(vr[h], l)
        for k in range(2):
            vr[k] = vr[k] - col * mod[k]
        for k in range(2):
            vr[k, pl.ds(j, 1), :] = norm[k]

    seg = 64
    carry = chol_step(0, 0, 0)
    for s in range(W // seg):
        h = s * seg // H
        start = s * seg

        def body(j, carry, h=h, start=start):
            new = chol_step(j, h, start)
            jordan_step(j - 1, h, carry)
            return new

        first = start
        if start % H == 0:
            if s > 0:
                new = chol_step(start, h, start)
                jordan_step(start - 1, h - 1, carry)
                carry = new
            first += 1
        carry = lax.fori_loop(first, start + seg, body, carry)
    jordan_step(W - 1, 1, carry)
    unroot = 1.0 / root
    for k in range(2):
        lt_ref[:, k * H : (k + 1) * H] = lt[k] * unroot
        tt_ref[:, k * H : (k + 1) * H] = vr[k] * scale


def factor(gram, top):
    vmem = pl.BlockSpec(memory_space=pltpu.VMEM)
    return pl.pallas_call(
        factor_kernel,
        out_shape=[jax.ShapeDtypeStruct((W, W), jnp.float32)] * 2,
        in_specs=[vmem] * 2,
        out_specs=[vmem] * 2,
        scratch_shapes=[pltpu.VMEM((2, W, H), jnp.float32)] * 3,
        cost_estimate=pl.CostEstimate(flops=2 * W**3, bytes_accessed=16 * W * W, transcendentals=0),
    )(gram, top)


def to_tiles(x):
    rows, cols = x.shape
    return x.reshape(rows // 8, 8, cols // H, H).transpose(0, 2, 1, 3).reshape(rows * cols // (8 * H), 8, H)


def from_tiles(x, rows, cols):
    return x.reshape(rows // 8, cols // H, 8, H).transpose(0, 2, 1, 3).reshape(rows, cols)


def sum_all(x, axes, parts):
    pieces = x.reshape((parts, -1) + x.shape[1:])
    mine = jnp.sum(lax.all_to_all(pieces, axes, 0, 0, tiled=True), axis=0)
    full = lax.all_to_all(jnp.broadcast_to(mine[None], (parts,) + mine.shape), axes, 0, 0, tiled=True)
    return full.reshape(x.shape)


def split(x):
    high = x.astype(jnp.bfloat16)
    return high, (x - high.astype(jnp.float32)).astype(jnp.bfloat16)


def dot3(a, b, contract):
    dims = (contract, ((), ()))
    a_high, a_low = split(a)
    b_high, b_low = split(b)

    def dot(x, y):
        return lax.dot_general(x, y, dims, preferred_element_type=jnp.float32)

    return dot(a_high, b_high) + (dot(a_high, b_low) + dot(a_low, b_high))


NN = ((1,), (0,))
NT = ((1,), (1,))
VMEM_BYTES = 50 * 1024 * 1024


def product_kernel(place_ref, a_ref, cols_ref, rows_ref, lt_ref, out_ref, inner_ref, acc):
    step = pl.program_id(0)
    steps = pl.num_programs(0)
    lower = lt_ref[...].T

    @pl.when(step == 0)
    def _():
        own = (place_ref[1] == 0).astype(jnp.float32)
        first = cols_ref[0, :, :W] + own * lower
        rest = cols_ref[0, :, W:]
        acc[...] = dot3(a_ref[:, :W], first, NT) + dot3(a_ref[:, W:], rest, NT)

    @pl.when(step > 0)
    def _():
        acc[...] += dot3(a_ref[...], cols_ref[0], NT)

    @pl.when(step == steps - 1)
    def _():
        total = acc[...]
        out_ref[...] = total
        own = (place_ref[0] == 0).astype(jnp.float32)
        inner = dot3(rows_ref[:, :W] + own * lower, total[:W], NN)
        inner_ref[...] = inner + dot3(rows_ref[:, W:], total[W:], NN)


def product(place, trailing, panel_cols, panel_rows, factor_t):
    rows, cols = trailing.shape
    half = panel_cols.shape[2]
    tile = 640
    per = half // tile
    return pl.pallas_call(
        product_kernel,
        grid=(cols // tile,),
        out_shape=[jax.ShapeDtypeStruct((rows, W), jnp.float32), jax.ShapeDtypeStruct((W, W), jnp.float32)],
        in_specs=[
            pl.BlockSpec(memory_space=pltpu.SMEM),
            pl.BlockSpec((rows, tile), lambda i: (0, i)),
            pl.BlockSpec((1, W, tile), lambda i: (i // per, 0, i % per)),
            pl.BlockSpec((W, rows), lambda i: (0, 0)),
            pl.BlockSpec((W, W), lambda i: (0, 0)),
        ],
        out_specs=[pl.BlockSpec((rows, W), lambda i: (0, 0)), pl.BlockSpec((W, W), lambda i: (0, 0))],
        scratch_shapes=[pltpu.VMEM((rows, W), jnp.float32)],
        compiler_params=pltpu.CompilerParams(vmem_limit_bytes=VMEM_BYTES),
        cost_estimate=pl.CostEstimate(flops=6 * rows * cols * W, bytes_accessed=4 * rows * cols, transcendentals=0),
    )(place, trailing, panel_cols, panel_rows, factor_t)


def update_kernel(place_ref, a_ref, cols_ref, wcols_ref, rows_ref, wrows_ref, lt_ref, tt_ref, inner_ref, out_ref,
                  half_ref, vh, vl, zh, zl):
    step = pl.program_id(0)

    def dot(x, y, contract):
        return lax.dot_general(x, y, (contract, ((), ())), preferred_element_type=jnp.float32)

    @pl.when(step == 0)
    def _():
        t = tt_ref[...]
        mid = jnp.dot(t, inner_ref[...], precision=HIGHEST, preferred_element_type=jnp.float32)
        half_ref[...] = 0.5 * lax.dot_general(mid, t, (NT, ((), ())), precision=HIGHEST, preferred_element_type=jnp.float32)
        own = (place_ref[0] == 0).astype(jnp.float32)
        lt = lt_ref[...] * own
        reflect = rows_ref[...].T
        vh[...], vl[...] = split(reflect)
        vh[:W], vl[:W] = split(reflect[:W] + lt)
        zh[...], zl[...] = split(wrows_ref[...] - dot3(reflect, half_ref[...], NN))
        zh[:W], zl[:W] = split(wrows_ref[:W] - dot3(reflect[:W] + lt, half_ref[...], NN))

    own = jnp.logical_and(place_ref[1] == 0, step == 0).astype(jnp.float32)
    lower = lt_ref[...].T * own
    cols = cols_ref[0]
    if cols.shape[1] > W:
        cols = jnp.concatenate([cols[:, :W] + lower, cols[:, W:]], axis=1)
    else:
        cols = cols + lower
    ch, cl = split(cols)
    fix = dot3(half_ref[...], cols, NN)
    weights = wcols_ref[...].T - fix
    wh, wl = split(weights)
    first = dot(vh[...], wh, NN) + (dot(vh[...], wl, NN) + dot(vl[...], wh, NN))
    second = dot(zh[...], ch, NN) + (dot(zh[...], cl, NN) + dot(zl[...], ch, NN))
    out_ref[...] = a_ref[...] - first - second


def update(place, trailing, panel_cols, weight_cols, panel_rows, weight_rows, factor_t, coupling_t, inner):
    rows, cols = trailing.shape
    half = panel_cols.shape[2]
    tile = 256
    per = half // tile
    square = pl.BlockSpec((W, W), lambda i: (0, 0))
    return pl.pallas_call(
        update_kernel,
        grid=(cols // tile,),
        out_shape=jax.ShapeDtypeStruct((rows, cols), jnp.float32),
        in_specs=[
            pl.BlockSpec(memory_space=pltpu.SMEM),
            pl.BlockSpec((rows, tile), lambda i: (0, i)),
            pl.BlockSpec((1, W, tile), lambda i: (i // per, 0, i % per)),
            pl.BlockSpec((tile, W), lambda i: (i, 0)),
            pl.BlockSpec((W, rows), lambda i: (0, 0)),
            pl.BlockSpec((rows, W), lambda i: (0, 0)),
            square,
            square,
            square,
        ],
        out_specs=pl.BlockSpec((rows, tile), lambda i: (0, i)),
        scratch_shapes=[pltpu.VMEM((W, W), jnp.float32)] + [pltpu.VMEM((rows, W), jnp.bfloat16)] * 4,
        compiler_params=pltpu.CompilerParams(vmem_limit_bytes=VMEM_BYTES),
        cost_estimate=pl.CostEstimate(flops=12 * rows * cols * W, bytes_accessed=8 * rows * cols, transcendentals=0),
    )(place, trailing, panel_cols, weight_cols, panel_rows, weight_rows, factor_t, coupling_t, inner)


def shards(trailing, panel_block):
    r = lax.axis_index("row")
    c = lax.axis_index("col")
    nr = lax.axis_size("row")
    nc = lax.axis_size("col")
    ratio = nr // nc
    perm = [(i * nc + j, ((i % ratio) * nc + j) * nc + i // ratio) for i in range(nr) for j in range(nc)]
    pair = [(j, j ^ 1) for j in range(nc)]
    lines = [list(range(k, nc, 2)) for k in range(2)]
    place = jnp.stack([r, c]).astype(jnp.int32)
    rows, width = panel_block.shape
    part = rows // nc
    panel_t = panel_block.T
    moved = lax.ppermute(panel_t, BOTH, perm)
    line = lax.all_gather(panel_t, "col", axis=0, axis_index_groups=lines)
    other = lax.ppermute(line, "col", pair)
    even = c % 2 == 0
    panel_rows = jnp.stack([jnp.where(even, line, other), jnp.where(even, other, line)], axis=1).reshape(W, rows)
    panel_cols = lax.all_gather(moved, "row", axis=0, tiled=True).reshape(ratio, W, rows)
    strip = lax.dot_general(panel_t, panel_rows, (((1,), (1,)), ((), ())), precision=HIGHEST)
    top = jnp.where(r == 0, panel_t[:, :W], jnp.zeros((width, W), jnp.float32))
    pieces = to_tiles(jnp.concatenate([strip, top], axis=1))
    mine = jnp.sum(lax.all_to_all(pieces, "row", 0, 0, tiled=True), axis=0)
    full = lax.all_to_all(jnp.broadcast_to(mine[None], (nr * nc,) + mine.shape), BOTH, 0, 0, tiled=True)
    tr, tc = width // 8, 2 * W // H
    full = full.reshape(tr, tc, nc, 8, H).transpose(2, 0, 3, 1, 4).reshape(W, 2 * W)
    factor_t, coupling_t = factor(full[:, :W], full[:, W:].T)
    partial, inner = product(place, trailing, panel_cols, panel_rows, factor_t)
    pieces = lax.all_to_all(partial.reshape(nc, part, W), "col", 0, 0, tiled=True)
    mine = jnp.sum(pieces, axis=0)
    mine = lax.dot_general(mine, coupling_t, (((1,), (1,)), ((), ())), precision=HIGHEST)
    moved = lax.ppermute(mine, BOTH, perm)
    weight_cols = lax.all_gather(moved, "row", axis=0, tiled=True)
    weight_rows = lax.all_gather(mine, "col", axis=0, tiled=True)
    inner = from_tiles(sum_all(to_tiles(inner).reshape(nr * nc, 4, H), BOTH, nr * nc).reshape(-1, 8, H), W, W)
    return update(place, trailing, panel_cols, weight_cols, panel_rows, weight_rows, factor_t, coupling_t, inner)


def solution(mesh):
    return jax.shard_map(shards, mesh=mesh, in_specs=(P("row", "col"), P("row", "col")), out_specs=P("row", "col"), check_vma=False)
```

```python
import jax
import jax.numpy as jnp
from jax import lax
from jax.experimental import pallas as pl
from jax.experimental.pallas import tpu as pltpu
from jax.sharding import PartitionSpec as P

W = 256
H = 128
BOTH = ("row", "col")
HIGHEST = lax.Precision.HIGHEST
HIGH = lax.Precision.HIGH


def lane(x, l):
    if x.shape[0] == 1:
        return lane(jnp.broadcast_to(x, (8, H)), l)[0:1]
    return jnp.take_along_axis(x, jnp.full(x.shape, l, jnp.int32), axis=1, mode="promise_in_bounds")


def factor_kernel(gram_ref, top_ref, lt_ref, tt_ref, gw, vr, lt, lw):
    ri = lax.broadcasted_iota(jnp.int32, (W, W), 0)
    ci = lax.broadcasted_iota(jnp.int32, (W, W), 1)
    li = lax.broadcasted_iota(jnp.int32, (1, H), 1)
    g = gram_ref[...]
    scale = 1.0 / jnp.max(jnp.where(ri == ci, g, 0.0), keepdims=True)
    root = jnp.sqrt(scale)
    t = top_ref[...] * root
    g = g * scale

    def dot(x, y):
        return jnp.dot(x, y, precision=HIGHEST, preferred_element_type=jnp.float32)

    def chol_step(j, row):
        here = li == j
        d = lane(row, j)
        rs = lax.rsqrt(d)
        rs = rs * (1.5 - 0.5 * d * rs * rs)
        inv = rs * rs
        mod = jnp.where(here, 1.0 + inv, row * inv)
        old = gw[pl.ds(jnp.minimum(j + 1, H - 1), 1), :]
        ahead = old - lane(old, j) * mod
        gw[...] = gw[...] - lane(gw[...], j) * mod
        scaled = row * rs
        lt[pl.ds(j, 1), :] = jnp.where(li >= j, scaled, 0.0)
        lw[pl.ds(j, 1), :] = jnp.where(here, rs, jnp.where(li < j, scaled, 0.0))
        return ahead, rs, scaled

    def jordan_step(j, row, rs, scaled):
        here = li == j
        row = row + scaled
        q = 1.0 / lane(row, j)
        norm = row * q
        rq = rs * q
        mod = jnp.where(here, 1.0 + rq, norm)
        old = vr[pl.ds(jnp.minimum(j + 1, H - 1), 1), :]
        ahead = old - lane(old, j) * mod
        vr[...] = vr[...] - lane(vr[...], j) * mod
        vr[pl.ds(j, 1), :] = jnp.where(here, rq, norm)
        return ahead

    def block(gram, top):
        gw[...] = gram
        vr[...] = top

        def body(j, carry):
            row, rs, scaled, vrow = carry
            new = chol_step(j, row)
            vrow = jordan_step(j - 1, vrow, rs, scaled)
            return new + (vrow,)

        carry = chol_step(0, gram[0:1]) + (top[0:1],)
        row, rs, scaled, vrow = lax.fori_loop(1, H, body, carry)
        jordan_step(H - 1, vrow, rs, scaled)
        return lt[...], lw[...], vr[...]

    g12, g22 = g[:H, H:], g[H:, H:]
    l11t, w11, x11 = block(g[:H, :H], t[:H, :H])
    l21t = dot(w11, g12)
    l21 = l21t.T
    inv11 = dot(x11, l11t.T)
    v12 = t[:H, H:] + l21t
    k21 = dot(t[H:, :H], inv11)
    n12 = dot(inv11, v12)
    l22t, w22, x22 = block(g22 - dot(l21, l21t), t[H:, H:] - dot(k21, v12))
    t21 = -dot(x22, dot(l21 + dot(l22t.T, k21), w11))
    unroot = 1.0 / root
    lt_ref[:H, :H] = l11t * unroot
    lt_ref[:H, H:] = l21t * unroot
    lt_ref[H:, :H] = jnp.zeros((H, H), jnp.float32)
    lt_ref[H:, H:] = l22t * unroot
    tt_ref[:H, :H] = (x11 - dot(n12, t21)) * scale
    tt_ref[:H, H:] = -dot(n12, x22) * scale
    tt_ref[H:, :H] = t21 * scale
    tt_ref[H:, H:] = x22 * scale


def factor(gram, top):
    vmem = pl.BlockSpec(memory_space=pltpu.VMEM)
    return pl.pallas_call(
        factor_kernel,
        out_shape=[jax.ShapeDtypeStruct((W, W), jnp.float32)] * 2,
        in_specs=[vmem] * 2,
        out_specs=[vmem] * 2,
        scratch_shapes=[pltpu.VMEM((H, H), jnp.float32)] * 4,
        cost_estimate=pl.CostEstimate(flops=2 * W**3, bytes_accessed=16 * W * W, transcendentals=0),
    )(gram, top)


def to_tiles(x):
    rows, cols = x.shape
    return x.reshape(rows // 8, 8, cols // H, H).transpose(0, 2, 1, 3).reshape(rows * cols // (8 * H), 8, H)


def from_tiles(x, rows, cols):
    return x.reshape(rows // 8, cols // H, 8, H).transpose(0, 2, 1, 3).reshape(rows, cols)


def sum_all(x, axes, parts):
    pieces = x.reshape((parts, -1) + x.shape[1:])
    mine = jnp.sum(lax.all_to_all(pieces, axes, 0, 0, tiled=True), axis=0)
    full = lax.all_to_all(jnp.broadcast_to(mine[None], (parts,) + mine.shape), axes, 0, 0, tiled=True)
    return full.reshape(x.shape)


def split(x):
    high = x.astype(jnp.bfloat16)
    return high, (x - high.astype(jnp.float32)).astype(jnp.bfloat16)


NN = ((1,), (0,))
NT = ((1,), (1,))
VMEM_BYTES = 50 * 1024 * 1024


def stack3(a, b, axis):
    a_high, a_low = split(a)
    b_high, b_low = split(b)
    return jnp.concatenate([a_high, a_high, a_low], axis=axis[0]), jnp.concatenate([b_high, b_low, b_high], axis=axis[1])


def dots(a, b, contract):
    left, right = stack3(a, b, (contract[0][0], contract[1][0]))
    return lax.dot_general(left, right, (contract, ((), ())), preferred_element_type=jnp.float32)


def product_kernel(place_ref, a_ref, cols_ref, rows_ref, lt_ref, out_ref, inner_ref, acc):
    step = pl.program_id(0)
    steps = pl.num_programs(0)
    lower = lt_ref[...].T

    @pl.when(step == 0)
    def _():
        own = (place_ref[1] == 0).astype(jnp.float32)
        first = cols_ref[0, :, :W] + own * lower
        rest = cols_ref[0, :, W:]
        acc[...] = dots(a_ref[:, :W], first, NT) + dots(a_ref[:, W:], rest, NT)

    @pl.when(step > 0)
    def _():
        acc[...] += dots(a_ref[...], cols_ref[0], NT)

    @pl.when(step == steps - 1)
    def _():
        total = acc[...]
        out_ref[...] = total
        own = (place_ref[0] == 0).astype(jnp.float32)
        inner = dots(rows_ref[:, :W] + own * lower, total[:W], NN)
        inner_ref[...] = inner + dots(rows_ref[:, W:], total[W:], NN)


def product(place, trailing, panel_cols, panel_rows, factor_t):
    rows, cols = trailing.shape
    half = panel_cols.shape[2]
    tile = 640
    per = half // tile
    return pl.pallas_call(
        product_kernel,
        grid=(cols // tile,),
        out_shape=[jax.ShapeDtypeStruct((rows, W), jnp.float32), jax.ShapeDtypeStruct((W, W), jnp.float32)],
        in_specs=[
            pl.BlockSpec(memory_space=pltpu.SMEM),
            pl.BlockSpec((rows, tile), lambda i: (0, i)),
            pl.BlockSpec((1, W, tile), lambda i: (i // per, 0, i % per)),
            pl.BlockSpec((W, rows), lambda i: (0, 0)),
            pl.BlockSpec((W, W), lambda i: (0, 0)),
        ],
        out_specs=[pl.BlockSpec((rows, W), lambda i: (0, 0)), pl.BlockSpec((W, W), lambda i: (0, 0))],
        scratch_shapes=[pltpu.VMEM((rows, W), jnp.float32)],
        compiler_params=pltpu.CompilerParams(vmem_limit_bytes=VMEM_BYTES),
        cost_estimate=pl.CostEstimate(flops=6 * rows * cols * W, bytes_accessed=4 * rows * cols, transcendentals=0),
    )(place, trailing, panel_cols, panel_rows, factor_t)


def prepare_kernel(place_ref, cols_ref, rows_ref, wrows_ref, lt_ref, tt_ref, inner_ref, left_ref, right_ref):
    t = tt_ref[...]
    mid = jnp.dot(t, inner_ref[...], precision=HIGHEST, preferred_element_type=jnp.float32)
    square = lax.dot_general(mid, t, (NT, ((), ())), precision=HIGHEST, preferred_element_type=jnp.float32)
    own_rows = (place_ref[0] == 0).astype(jnp.float32)
    own_cols = (place_ref[1] == 0).astype(jnp.float32)
    lt = lt_ref[...]
    for i in range(rows_ref.shape[1] // W):
        at = slice(i * W, (i + 1) * W)
        reflect = rows_ref[:, at].T
        if i == 0:
            reflect = reflect + lt * own_rows
        weights = wrows_ref[at] - dots(reflect, square, NN)
        for k, x in enumerate((reflect, weights)):
            high, low = split(x)
            for p, part in enumerate((high, high, low)):
                left_ref[at, (3 * k + p) * W : (3 * k + p + 1) * W] = part
    half = cols_ref.shape[2]
    for h in range(cols_ref.shape[0]):
        for i in range(half // W):
            cols = cols_ref[h, :, i * W : (i + 1) * W]
            if h == 0 and i == 0:
                cols = cols + lt.T * own_cols
            high, low = split(cols)
            at = slice(h * half + i * W, h * half + (i + 1) * W)
            for p, part in enumerate((high, low, high)):
                right_ref[p * W : (p + 1) * W, at] = part


def prepare(place, panel_cols, panel_rows, weight_rows, factor_t, coupling_t, inner):
    rows = panel_rows.shape[1]
    cols = panel_cols.shape[0] * panel_cols.shape[2]
    vmem = pl.BlockSpec(memory_space=pltpu.VMEM)
    return pl.pallas_call(
        prepare_kernel,
        out_shape=[jax.ShapeDtypeStruct((rows, 6 * W), jnp.bfloat16), jax.ShapeDtypeStruct((3 * W, cols), jnp.bfloat16)],
        in_specs=[pl.BlockSpec(memory_space=pltpu.SMEM)] + [vmem] * 6,
        out_specs=[vmem] * 2,
        compiler_params=pltpu.CompilerParams(vmem_limit_bytes=VMEM_BYTES),
        cost_estimate=pl.CostEstimate(flops=6 * rows * W * W, bytes_accessed=16 * rows * W, transcendentals=0),
    )(place, panel_cols, panel_rows, weight_rows, factor_t, coupling_t, inner)


def update_kernel(a_ref, left_ref, right_ref, weights_ref, out_ref):
    high, low = split(weights_ref[...].T)
    right = jnp.concatenate([high, low, high], axis=0)
    first = jnp.dot(left_ref[:, : 3 * W], right, preferred_element_type=jnp.float32)
    second = jnp.dot(left_ref[:, 3 * W :], right_ref[...], preferred_element_type=jnp.float32)
    out_ref[...] = a_ref[...] - (first + second)


def update(trailing, left, right, weight_cols):
    rows, cols = trailing.shape
    tile = 512
    return pl.pallas_call(
        update_kernel,
        grid=(cols // tile,),
        out_shape=jax.ShapeDtypeStruct((rows, cols), jnp.float32),
        in_specs=[
            pl.BlockSpec((rows, tile), lambda i: (0, i)),
            pl.BlockSpec((rows, 6 * W), lambda i: (0, 0)),
            pl.BlockSpec((3 * W, tile), lambda i: (0, i)),
            pl.BlockSpec((tile, W), lambda i: (i, 0)),
        ],
        out_specs=pl.BlockSpec((rows, tile), lambda i: (0, i)),
        compiler_params=pltpu.CompilerParams(vmem_limit_bytes=VMEM_BYTES),
        cost_estimate=pl.CostEstimate(flops=12 * rows * cols * W, bytes_accessed=8 * rows * cols, transcendentals=0),
    )(trailing, left, right, weight_cols)


def shards(trailing, panel_block):
    r = lax.axis_index("row")
    c = lax.axis_index("col")
    nr = lax.axis_size("row")
    nc = lax.axis_size("col")
    ratio = nr // nc
    perm = [(i * nc + j, ((i % ratio) * nc + j) * nc + i // ratio) for i in range(nr) for j in range(nc)]
    pair = [(j, j ^ 1) for j in range(nc)]
    lines = [list(range(k, nc, 2)) for k in range(2)]
    place = jnp.stack([r, c]).astype(jnp.int32)
    rows, width = panel_block.shape
    part = rows // nc
    panel_t = panel_block.T

    def gather_col(x):
        line = lax.all_gather(x, "col", axis=0, axis_index_groups=lines)
        other = lax.ppermute(line, "col", pair)
        even = c % 2 == 0
        both = jnp.stack([jnp.where(even, line, other), jnp.where(even, other, line)], axis=1)
        return both.reshape((-1,) + x.shape[1:])

    panel_rows = gather_col(panel_t)
    panel_rows, later = lax.optimization_barrier((panel_rows, panel_t))
    moved = lax.ppermute(later, BOTH, perm)
    panel_cols = lax.all_gather(moved, "row", axis=0, tiled=True).reshape(ratio, W, rows)
    strip = lax.dot_general(panel_t, panel_rows, (((1,), (1,)), ((), ())), precision=HIGHEST)
    top = jnp.where(r == 0, panel_t[:, :W], jnp.zeros((width, W), jnp.float32))
    pieces = to_tiles(jnp.concatenate([strip, top], axis=1))
    mine = jnp.sum(lax.all_to_all(pieces, "row", 0, 0, tiled=True), axis=0)
    full = lax.all_to_all(jnp.broadcast_to(mine[None], (nr * nc,) + mine.shape), BOTH, 0, 0, tiled=True)
    tr, tc = width // 8, 2 * W // H
    full = full.reshape(tr, tc, nc, 8, H).transpose(2, 0, 3, 1, 4).reshape(W, 2 * W)
    factor_t, coupling_t = factor(full[:, :W], full[:, W:].T)
    partial, inner = product(place, trailing, panel_cols, panel_rows, factor_t)
    pieces = lax.all_to_all(partial.reshape(nc, part, W), "col", 0, 0, tiled=True)
    mine = jnp.sum(pieces, axis=0)
    mine = lax.dot_general(mine, coupling_t, (((1,), (1,)), ((), ())), precision=HIGHEST)
    moved = lax.ppermute(mine, BOTH, perm)
    weight_cols = lax.all_gather(moved, "row", axis=0, tiled=True)
    weight_rows = gather_col(mine)
    inner = from_tiles(sum_all(to_tiles(inner).reshape(nr * nc, 4, H), BOTH, nr * nc).reshape(-1, 8, H), W, W)
    left, right = prepare(place, panel_cols, panel_rows, weight_rows, factor_t, coupling_t, inner)
    return update(trailing, left, right, weight_cols)


def solution(mesh):
    return jax.shard_map(shards, mesh=mesh, in_specs=(P("row", "col"), P("row", "col")), out_specs=P("row", "col"), check_vma=False)
```

```python
import jax
import jax.numpy as jnp
from jax import lax
from jax.experimental import pallas as pl
from jax.experimental.pallas import tpu as pltpu
from jax.sharding import PartitionSpec as P

W = 256
H = 128
PANEL = 8
BOTH = ("row", "col")
HIGHEST = lax.Precision.HIGHEST


def lane(x, l):
    if x.shape[0] == 1:
        return lane(jnp.broadcast_to(x, (8, H)), l)[0:1]
    return jnp.take_along_axis(x, jnp.full(x.shape, l, jnp.int32), axis=1, mode="promise_in_bounds")


def panel_step(solo, rows, at):
    li = lax.broadcasted_iota(jnp.int32, (1, H), 1)
    sub = lax.broadcasted_iota(jnp.int32, (PANEL, H), 0)
    cols = [lane(rows, at + k) for k in range(PANEL)]
    mods, ratios, marks = [], [], []
    for a in range(PANEL):
        here = li == at + a
        row = rows[a : a + 1]
        tops = [cols[k][a : a + 1] for k in range(PANEL)]
        mod, ratio, final, mark = solo(a, here, row, tops)
        mods.append(mod)
        ratios.append(ratio)
        marks.append(mark)
        own = sub == a
        rows = jnp.where(own, final, rows - cols[a] * mod)
        for k in range(a + 1, PANEL):
            cols[k] = jnp.where(own, ratio[k], cols[k] - cols[a] * ratio[k])
    for a in range(PANEL - 2, -1, -1):
        for k in range(a + 1, PANEL):
            mods[a] = mods[a] - ratios[a][k] * mods[k]
    return rows, mods, marks


def update_rows(mat, cols, mods):
    new = mat[...]
    for col, mod in zip(cols, mods):
        new = new - col * mod
    mat[...] = new


def factor_kernel(gram_ref, top_ref, lt_ref, tt_ref, gw, vr, lt, lw, spread):
    ri = lax.broadcasted_iota(jnp.int32, (W, W), 0)
    ci = lax.broadcasted_iota(jnp.int32, (W, W), 1)
    li = lax.broadcasted_iota(jnp.int32, (1, H), 1)
    g = gram_ref[...]
    scale = 1.0 / jnp.max(jnp.where(ri == ci, g, 0.0), keepdims=True)
    root = jnp.sqrt(scale)
    t = top_ref[...] * root
    g = g * scale

    def dot(x, y):
        return jnp.dot(x, y, precision=HIGHEST, preferred_element_type=jnp.float32)

    def chol_panel(at):
        old = [lane(gw[...], at + k) for k in range(PANEL)]

        def solo(a, here, row, tops):
            d = tops[a]
            inv = 1.0 / d
            rs = lax.rsqrt(d)
            rs = rs * (1.5 - 0.5 * d * rs * rs)
            scaled = row * rs
            mod = jnp.where(here, 1.0 + inv, row * inv)
            ratio = [top * inv for top in tops]
            upper = jnp.where(li >= at + a, scaled, 0.0)
            lower = jnp.where(here, rs, jnp.where(li < at + a, scaled, 0.0))
            marks = [rs, scaled] + [top * rs for top in tops]
            return mod, ratio, row, (upper, lower, marks)

        _, mods, marks = panel_step(solo, gw[pl.ds(at, PANEL), :], at)
        update_rows(gw, old, mods)
        lt[pl.ds(at, PANEL), :] = jnp.concatenate([m[0] for m in marks], axis=0)
        lw[pl.ds(at, PANEL), :] = jnp.concatenate([m[1] for m in marks], axis=0)
        for a in range(PANEL):
            for i, x in enumerate(marks[a][2]):
                if i < 2 or i - 2 >= a:
                    spread[a, i : i + 1, :] = x

    def jordan_panel(at):
        old = [lane(vr[...], at + k) for k in range(PANEL)]
        marks = [[spread[a, i : i + 1, :] for i in range(PANEL + 2)] for a in range(PANEL)]

        def solo(a, here, row, tops):
            rs, scaled = marks[a][:2]
            row = row + scaled
            q = 1.0 / (tops[a] + marks[a][2 + a])
            norm = row * q
            rq = rs * q
            mod = jnp.where(here, 1.0 + rq, norm)
            final = jnp.where(here, rq, norm)
            ratio = [(tops[k] + marks[a][2 + k]) * q if k > a else None for k in range(PANEL)]
            return mod, ratio, final, None

        rows, mods, _ = panel_step(solo, vr[pl.ds(at, PANEL), :], at)
        update_rows(vr, old, mods)
        vr[pl.ds(at, PANEL), :] = rows

    def block(gram, top):
        gw[...] = gram
        vr[...] = top
        chol_panel(0)

        def body(i, _):
            at = pl.multiple_of(i * PANEL, PANEL)
            jordan_panel(at - PANEL)
            chol_panel(at)
            return 0

        lax.fori_loop(1, H // PANEL, body, 0)
        jordan_panel(H - PANEL)
        return lt[...], lw[...], vr[...]

    g12, g22 = g[:H, H:], g[H:, H:]
    l11t, w11, x11 = block(g[:H, :H], t[:H, :H])
    l21t = dot(w11, g12)
    l21 = l21t.T
    inv11 = dot(x11, l11t.T)
    v12 = t[:H, H:] + l21t
    k21 = dot(t[H:, :H], inv11)
    n12 = dot(inv11, v12)
    l22t, w22, x22 = block(g22 - dot(l21, l21t), t[H:, H:] - dot(k21, v12))
    t21 = -dot(x22, dot(l21 + dot(l22t.T, k21), w11))
    unroot = 1.0 / root
    lt_ref[:H, :H] = l11t * unroot
    lt_ref[:H, H:] = l21t * unroot
    lt_ref[H:, :H] = jnp.zeros((H, H), jnp.float32)
    lt_ref[H:, H:] = l22t * unroot
    tt_ref[:H, :H] = (x11 - dot(n12, t21)) * scale
    tt_ref[:H, H:] = -dot(n12, x22) * scale
    tt_ref[H:, :H] = t21 * scale
    tt_ref[H:, H:] = x22 * scale


def factor(gram, top):
    vmem = pl.BlockSpec(memory_space=pltpu.VMEM)
    return pl.pallas_call(
        factor_kernel,
        out_shape=[jax.ShapeDtypeStruct((W, W), jnp.float32)] * 2,
        in_specs=[vmem] * 2,
        out_specs=[vmem] * 2,
        scratch_shapes=[pltpu.VMEM((H, H), jnp.float32)] * 4 + [pltpu.VMEM((PANEL, PANEL + 2, H), jnp.float32)],
        cost_estimate=pl.CostEstimate(flops=2 * W**3, bytes_accessed=16 * W * W, transcendentals=0),
    )(gram, top)


def to_tiles(x):
    rows, cols = x.shape
    return x.reshape(rows // 8, 8, cols // H, H).transpose(0, 2, 1, 3).reshape(rows * cols // (8 * H), 8, H)


def from_tiles(x, rows, cols):
    return x.reshape(rows // 8, cols // H, 8, H).transpose(0, 2, 1, 3).reshape(rows, cols)


def split(x):
    high = x.astype(jnp.bfloat16)
    return high, (x - high.astype(jnp.float32)).astype(jnp.bfloat16)


NN = ((1,), (0,))
NT = ((1,), (1,))
VMEM_BYTES = 50 * 1024 * 1024


def stack3(a, b, axis):
    a_high, a_low = split(a)
    b_high, b_low = split(b)
    return jnp.concatenate([a_high, a_high, a_low], axis=axis[0]), jnp.concatenate([b_high, b_low, b_high], axis=axis[1])


def dots(a, b, contract):
    left, right = stack3(a, b, (contract[0][0], contract[1][0]))
    return lax.dot_general(left, right, (contract, ((), ())), preferred_element_type=jnp.float32)


def product_kernel(place_ref, a_ref, cols_ref, rows_ref, lt_ref, out_ref, acc):
    step = pl.program_id(0)
    steps = pl.num_programs(0)
    lower = lt_ref[...].T

    @pl.when(step == 0)
    def _():
        own = (place_ref[1] == 0).astype(jnp.float32)
        first = cols_ref[0, :, :W] + own * lower
        rest = cols_ref[0, :, W:]
        acc[...] = dots(a_ref[:, :W], first, NT) + dots(a_ref[:, W:], rest, NT)

    @pl.when(step > 0)
    def _():
        acc[...] += dots(a_ref[...], cols_ref[0], NT)

    @pl.when(step == steps - 1)
    def _():
        total = acc[...]
        own = (place_ref[0] == 0).astype(jnp.float32)
        inner = dots(rows_ref[:, :W] + own * lower, total[:W], NN)
        inner = inner + dots(rows_ref[:, W:], total[W:], NN)
        parts = out_ref.shape[0]
        part = total.shape[0] // parts
        for q in range(parts):
            out_ref[q, :part] = total[q * part : (q + 1) * part]
            out_ref[q, part:] = inner[q * W // parts : (q + 1) * W // parts]


def product(place, trailing, panel_cols, panel_rows, factor_t, parts):
    rows, cols = trailing.shape
    half = panel_cols.shape[2]
    tile = 640
    per = half // tile
    return pl.pallas_call(
        product_kernel,
        grid=(cols // tile,),
        out_shape=jax.ShapeDtypeStruct((parts, (rows + W) // parts, W), jnp.float32),
        in_specs=[
            pl.BlockSpec(memory_space=pltpu.SMEM),
            pl.BlockSpec((rows, tile), lambda i: (0, i)),
            pl.BlockSpec((1, W, tile), lambda i: (i // per, 0, i % per)),
            pl.BlockSpec((W, rows), lambda i: (0, 0)),
            pl.BlockSpec((W, W), lambda i: (0, 0)),
        ],
        out_specs=pl.BlockSpec((parts, (rows + W) // parts, W), lambda i: (0, 0, 0)),
        scratch_shapes=[pltpu.VMEM((rows, W), jnp.float32)],
        compiler_params=pltpu.CompilerParams(vmem_limit_bytes=VMEM_BYTES),
        cost_estimate=pl.CostEstimate(flops=6 * rows * cols * W, bytes_accessed=4 * rows * cols, transcendentals=0),
    )(place, trailing, panel_cols, panel_rows, factor_t)


def prepare_kernel(place_ref, cols_ref, rows_ref, wrows_ref, lt_ref, tt_ref, inner_ref, left_ref, right_ref):
    t = tt_ref[...]
    mid = jnp.dot(t, inner_ref[...], precision=HIGHEST, preferred_element_type=jnp.float32)
    square = lax.dot_general(mid, t, (NT, ((), ())), precision=HIGHEST, preferred_element_type=jnp.float32)
    own_rows = (place_ref[0] == 0).astype(jnp.float32)
    own_cols = (place_ref[1] == 0).astype(jnp.float32)
    lt = lt_ref[...]
    for i in range(rows_ref.shape[1] // W):
        at = slice(i * W, (i + 1) * W)
        reflect = rows_ref[:, at].T
        if i == 0:
            reflect = reflect + lt * own_rows
        weights = wrows_ref[at] - dots(reflect, square, NN)
        for k, x in enumerate((reflect, weights)):
            high, low = split(x)
            for p, part in enumerate((high, high, low)):
                left_ref[at, (3 * k + p) * W : (3 * k + p + 1) * W] = part
    half = cols_ref.shape[2]
    for h in range(cols_ref.shape[0]):
        for i in range(half // W):
            cols = cols_ref[h, :, i * W : (i + 1) * W]
            if h == 0 and i == 0:
                cols = cols + lt.T * own_cols
            high, low = split(cols)
            at = slice(h * half + i * W, h * half + (i + 1) * W)
            for p, part in enumerate((high, low, high)):
                right_ref[p * W : (p + 1) * W, at] = part


def prepare(place, panel_cols, panel_rows, weight_rows, factor_t, coupling_t, inner):
    rows = panel_rows.shape[1]
    cols = panel_cols.shape[0] * panel_cols.shape[2]
    vmem = pl.BlockSpec(memory_space=pltpu.VMEM)
    return pl.pallas_call(
        prepare_kernel,
        out_shape=[jax.ShapeDtypeStruct((rows, 6 * W), jnp.bfloat16), jax.ShapeDtypeStruct((3 * W, cols), jnp.bfloat16)],
        in_specs=[pl.BlockSpec(memory_space=pltpu.SMEM)] + [vmem] * 6,
        out_specs=[vmem] * 2,
        compiler_params=pltpu.CompilerParams(vmem_limit_bytes=VMEM_BYTES),
        cost_estimate=pl.CostEstimate(flops=6 * rows * W * W, bytes_accessed=16 * rows * W, transcendentals=0),
    )(place, panel_cols, panel_rows, weight_rows, factor_t, coupling_t, inner)


def update_kernel(a_ref, left_ref, right_ref, weights_ref, out_ref):
    high, low = split(weights_ref[...].T)
    right = jnp.concatenate([high, low, high], axis=0)
    first = jnp.dot(left_ref[:, : 3 * W], right, preferred_element_type=jnp.float32)
    second = jnp.dot(left_ref[:, 3 * W :], right_ref[...], preferred_element_type=jnp.float32)
    out_ref[...] = a_ref[...] - (first + second)


def update(trailing, left, right, weight_cols):
    rows, cols = trailing.shape
    tile = 512
    return pl.pallas_call(
        update_kernel,
        grid=(cols // tile,),
        out_shape=jax.ShapeDtypeStruct((rows, cols), jnp.float32),
        in_specs=[
            pl.BlockSpec((rows, tile), lambda i: (0, i)),
            pl.BlockSpec((rows, 6 * W), lambda i: (0, 0)),
            pl.BlockSpec((3 * W, tile), lambda i: (0, i)),
            pl.BlockSpec((tile, W), lambda i: (i, 0)),
        ],
        out_specs=pl.BlockSpec((rows, tile), lambda i: (0, i)),
        compiler_params=pltpu.CompilerParams(vmem_limit_bytes=VMEM_BYTES),
        cost_estimate=pl.CostEstimate(flops=12 * rows * cols * W, bytes_accessed=8 * rows * cols, transcendentals=0),
    )(trailing, left, right, weight_cols)


def shards(trailing, panel_block):
    r = lax.axis_index("row")
    c = lax.axis_index("col")
    nr = lax.axis_size("row")
    nc = lax.axis_size("col")
    ratio = nr // nc
    perm = [(i * nc + j, ((i % ratio) * nc + j) * nc + i // ratio) for i in range(nr) for j in range(nc)]
    pair = [(j, j ^ 1) for j in range(nc)]
    lines = [list(range(k, nc, 2)) for k in range(2)]
    place = jnp.stack([r, c]).astype(jnp.int32)
    rows, width = panel_block.shape
    part = rows // nc
    panel_t = panel_block.T

    def gather_line(x):
        return lax.all_gather(x, "col", axis=0, axis_index_groups=lines)

    def join_cores(line):
        other = lax.ppermute(line, "col", pair)
        even = c % 2 == 0
        both = jnp.stack([jnp.where(even, line, other), jnp.where(even, other, line)], axis=1)
        return both.reshape((-1,) + line.shape[2:])

    moved = lax.ppermute(panel_t, BOTH, perm)
    line, moved = lax.optimization_barrier((gather_line(panel_t), moved))
    panel_rows = join_cores(line)
    panel_cols = lax.all_gather(moved, "row", axis=0, tiled=True).reshape(ratio, W, rows)
    strip = lax.dot_general(panel_t, panel_rows, (((1,), (1,)), ((), ())), precision=HIGHEST)
    top = jnp.where(r == 0, panel_t[:, :W], jnp.zeros((width, W), jnp.float32))
    pieces = to_tiles(jnp.concatenate([strip, top], axis=1))
    mine = jnp.sum(lax.all_to_all(pieces, "row", 0, 0, tiled=True), axis=0)
    full = lax.all_to_all(jnp.broadcast_to(mine[None], (nr * nc,) + mine.shape), BOTH, 0, 0, tiled=True)
    tr, tc = width // 8, 2 * W // H
    full = full.reshape(tr, tc, nc, 8, H).transpose(2, 0, 3, 1, 4).reshape(W, 2 * W)
    factor_t, coupling_t = factor(full[:, :W], full[:, W:].T)
    partial = product(place, trailing, panel_cols, panel_rows, factor_t, nc)
    pieces = jnp.sum(lax.all_to_all(partial, "col", 0, 0, tiled=True), axis=0)
    mine, inner = pieces[:part], pieces[part:]
    mine = lax.dot_general(mine, coupling_t, (((1,), (1,)), ((), ())), precision=HIGHEST)
    moved = lax.ppermute(mine, BOTH, perm)
    weight_cols = lax.all_gather(moved, "row", axis=0, tiled=True)
    weight_rows = join_cores(gather_line(mine))
    half = (nr, 8 * W * W // (8 * H * nr * nc), H)
    inner = jnp.sum(lax.all_to_all(to_tiles(inner).reshape(half), "row", 0, 0, tiled=True), axis=0)
    inner = jnp.broadcast_to(inner[None], (nr * nc,) + inner.shape)
    inner = lax.all_to_all(inner, BOTH, 0, 0, tiled=True).reshape((nr, nc) + inner.shape[1:])
    inner = from_tiles(inner.transpose(1, 0, 2, 3).reshape(-1, 8, H), W, W)
    left, right = prepare(place, panel_cols, panel_rows, weight_rows, factor_t, coupling_t, inner)
    return update(trailing, left, right, weight_cols)


def solution(mesh):
    return jax.shard_map(shards, mesh=mesh, in_specs=(P("row", "col"), P("row", "col")), out_specs=P("row", "col"), check_vma=False)
```

```python
import jax
import jax.numpy as jnp
from jax import lax
from jax.experimental import pallas as pl
from jax.experimental.pallas import tpu as pltpu
from jax.sharding import PartitionSpec as P

W = 256
H = 128
PANEL = 8
BOTH = ("row", "col")
HIGHEST = lax.Precision.HIGHEST


def lane(x, l):
    if x.shape[0] == 1:
        return lane(jnp.broadcast_to(x, (8, H)), l)[0:1]
    return jnp.take_along_axis(x, jnp.full(x.shape, l, jnp.int32), axis=1, mode="promise_in_bounds")


def panel_step(solo, rows, at):
    li = lax.broadcasted_iota(jnp.int32, (1, H), 1)
    sub = lax.broadcasted_iota(jnp.int32, (PANEL, H), 0)
    cols = [lane(rows, at + k) for k in range(PANEL)]
    mods, ratios, marks = [], [], []
    for a in range(PANEL):
        here = li == at + a
        row = rows[a : a + 1]
        tops = [cols[k][a : a + 1] for k in range(PANEL)]
        mod, ratio, final, mark = solo(a, here, row, tops)
        mods.append(mod)
        ratios.append(ratio)
        marks.append(mark)
        own = sub == a
        rows = jnp.where(own, final, rows - cols[a] * mod)
        for k in range(a + 1, PANEL):
            cols[k] = jnp.where(own, ratio[k], cols[k] - cols[a] * ratio[k])
    for a in range(PANEL - 2, -1, -1):
        for k in range(a + 1, PANEL):
            mods[a] = mods[a] - ratios[a][k] * mods[k]
    return rows, mods, marks


def update_rows(mat, cols, mods):
    new = mat[...]
    for col, mod in zip(cols, mods):
        new = new - col * mod
    mat[...] = new


def factor_kernel(gram_ref, top_ref, lt_ref, tt_ref, gw, vr, lt, lw, spread):
    ri = lax.broadcasted_iota(jnp.int32, (W, W), 0)
    ci = lax.broadcasted_iota(jnp.int32, (W, W), 1)
    li = lax.broadcasted_iota(jnp.int32, (1, H), 1)
    g = gram_ref[...]
    scale = 1.0 / jnp.max(jnp.where(ri == ci, g, 0.0), keepdims=True)
    root = jnp.sqrt(scale)
    t = top_ref[...] * root
    g = g * scale

    def dot(x, y):
        return jnp.dot(x, y, precision=HIGHEST, preferred_element_type=jnp.float32)

    def chol_panel(at):
        old = [lane(gw[...], at + k) for k in range(PANEL)]

        def solo(a, here, row, tops):
            d = tops[a]
            inv = 1.0 / d
            rs = lax.rsqrt(d)
            rs = rs * (1.5 - 0.5 * d * rs * rs)
            scaled = row * rs
            mod = jnp.where(here, 1.0 + inv, row * inv)
            ratio = [top * inv for top in tops]
            upper = jnp.where(li >= at + a, scaled, 0.0)
            lower = jnp.where(here, rs, jnp.where(li < at + a, scaled, 0.0))
            marks = [rs, scaled] + [top * rs for top in tops]
            return mod, ratio, row, (upper, lower, marks)

        _, mods, marks = panel_step(solo, gw[pl.ds(at, PANEL), :], at)
        update_rows(gw, old, mods)
        lt[pl.ds(at, PANEL), :] = jnp.concatenate([m[0] for m in marks], axis=0)
        lw[pl.ds(at, PANEL), :] = jnp.concatenate([m[1] for m in marks], axis=0)
        for a in range(PANEL):
            for i, x in enumerate(marks[a][2]):
                if i < 2 or i - 2 >= a:
                    spread[a, i : i + 1, :] = x

    def jordan_panel(at):
        old = [lane(vr[...], at + k) for k in range(PANEL)]
        marks = [[spread[a, i : i + 1, :] for i in range(PANEL + 2)] for a in range(PANEL)]

        def solo(a, here, row, tops):
            rs, scaled = marks[a][:2]
            row = row + scaled
            q = 1.0 / (tops[a] + marks[a][2 + a])
            norm = row * q
            rq = rs * q
            mod = jnp.where(here, 1.0 + rq, norm)
            final = jnp.where(here, rq, norm)
            ratio = [(tops[k] + marks[a][2 + k]) * q if k > a else None for k in range(PANEL)]
            return mod, ratio, final, None

        rows, mods, _ = panel_step(solo, vr[pl.ds(at, PANEL), :], at)
        update_rows(vr, old, mods)
        vr[pl.ds(at, PANEL), :] = rows

    def block(gram, top):
        gw[...] = gram
        vr[...] = top
        chol_panel(0)

        def body(i, _):
            at = pl.multiple_of(i * PANEL, PANEL)
            jordan_panel(at - PANEL)
            chol_panel(at)
            return 0

        lax.fori_loop(1, H // PANEL, body, 0)
        jordan_panel(H - PANEL)
        return lt[...], lw[...], vr[...]

    g12, g22 = g[:H, H:], g[H:, H:]
    l11t, w11, x11 = block(g[:H, :H], t[:H, :H])
    l21t = dot(w11, g12)
    l21 = l21t.T
    inv11 = dot(x11, l11t.T)
    v12 = t[:H, H:] + l21t
    k21 = dot(t[H:, :H], inv11)
    n12 = dot(inv11, v12)
    l22t, w22, x22 = block(g22 - dot(l21, l21t), t[H:, H:] - dot(k21, v12))
    t21 = -dot(x22, dot(l21 + dot(l22t.T, k21), w11))
    unroot = 1.0 / root
    lt_ref[:H, :H] = l11t * unroot
    lt_ref[:H, H:] = l21t * unroot
    lt_ref[H:, :H] = jnp.zeros((H, H), jnp.float32)
    lt_ref[H:, H:] = l22t * unroot
    tt_ref[:H, :H] = (x11 - dot(n12, t21)) * scale
    tt_ref[:H, H:] = -dot(n12, x22) * scale
    tt_ref[H:, :H] = t21 * scale
    tt_ref[H:, H:] = x22 * scale


def factor(gram, top):
    vmem = pl.BlockSpec(memory_space=pltpu.VMEM)
    return pl.pallas_call(
        factor_kernel,
        out_shape=[jax.ShapeDtypeStruct((W, W), jnp.float32)] * 2,
        in_specs=[vmem] * 2,
        out_specs=[vmem] * 2,
        scratch_shapes=[pltpu.VMEM((H, H), jnp.float32)] * 4 + [pltpu.VMEM((PANEL, PANEL + 2, H), jnp.float32)],
        cost_estimate=pl.CostEstimate(flops=2 * W**3, bytes_accessed=16 * W * W, transcendentals=0),
    )(gram, top)


def to_tiles(x):
    rows, cols = x.shape
    return x.reshape(rows // 8, 8, cols // H, H).transpose(0, 2, 1, 3).reshape(rows * cols // (8 * H), 8, H)


def from_tiles(x, rows, cols):
    return x.reshape(rows // 8, cols // H, 8, H).transpose(0, 2, 1, 3).reshape(rows, cols)


def split(x):
    high = x.astype(jnp.bfloat16)
    return high, (x - high.astype(jnp.float32)).astype(jnp.bfloat16)


NN = ((1,), (0,))
NT = ((1,), (1,))
VMEM_BYTES = 60 * 1024 * 1024


def dots(a, b, contract):
    a_high, a_low = split(a)
    b_high, b_low = split(b)
    left = jnp.concatenate([a_high, a_high, a_low], axis=contract[0][0])
    right = jnp.concatenate([b_high, b_low, b_high], axis=contract[1][0])
    return lax.dot_general(left, right, (contract, ((), ())), preferred_element_type=jnp.float32)


def product_kernel(place_ref, a_ref, cols_ref, rows_ref, lt_ref, keep_ref, send_ref, acc):
    step = pl.program_id(0)
    steps = pl.num_programs(0)

    @pl.when(step == 0)
    def _():
        own = (place_ref[1] == 0).astype(jnp.float32)
        cols = cols_ref[0]
        cols = jnp.concatenate([cols[:, :W] + own * lt_ref[...].T, cols[:, W:]], axis=1)
        acc[...] = dots(a_ref[...], cols, NT)

    @pl.when(step > 0)
    def _():
        acc[...] += dots(a_ref[...], cols_ref[0], NT)

    @pl.when(step == steps - 1)
    def _():
        own = (place_ref[0] == 0).astype(jnp.float32)
        inner = dots(rows_ref[:, :W] + own * lt_ref[...].T, acc[:W], NN)
        inner = inner + dots(rows_ref[:, W:], acc[W:], NN)
        odd = place_ref[1] % 2 == 1
        lines = keep_ref.shape[0]
        part = acc.shape[0] // (2 * lines)
        size = W // (2 * lines)
        for q in range(lines):
            for k in range(2):
                i = 2 * q + k
                for target, mine in ((keep_ref, odd == (k == 1)), (send_ref, odd != (k == 1))):

                    @pl.when(mine)
                    def _(target=target, i=i, q=q):
                        target[q, :part] = acc[i * part : (i + 1) * part]
                        target[q, part:] = inner[i * size : (i + 1) * size]


def product(place, trailing, panel_cols, panel_rows, factor_t, parts):
    rows, cols = trailing.shape
    half = panel_cols.shape[2]
    tile = 640
    per = half // tile
    out = jax.ShapeDtypeStruct((parts // 2, (rows + W) // parts, W), jnp.float32)
    out_spec = pl.BlockSpec(out.shape, lambda i: (0, 0, 0))
    return pl.pallas_call(
        product_kernel,
        grid=(cols // tile,),
        out_shape=[out, out],
        in_specs=[
            pl.BlockSpec(memory_space=pltpu.SMEM),
            pl.BlockSpec((rows, tile), lambda i: (0, i)),
            pl.BlockSpec((1, W, tile), lambda i: (i // per, 0, i % per)),
            pl.BlockSpec((W, rows), lambda i: (0, 0)),
            pl.BlockSpec((W, W), lambda i: (0, 0)),
        ],
        out_specs=[out_spec, out_spec],
        scratch_shapes=[pltpu.VMEM((rows, W), jnp.float32)],
        compiler_params=pltpu.CompilerParams(vmem_limit_bytes=VMEM_BYTES),
        cost_estimate=pl.CostEstimate(flops=6 * rows * cols * W, bytes_accessed=4 * rows * cols, transcendentals=0),
    )(place, trailing, panel_cols, panel_rows, factor_t)


def prepare_kernel(place_ref, cols_ref, rows_ref, own_ref, other_ref, lt_ref, tt_ref, inner_ref, out_ref, right_ref, reflect):
    half = cols_ref.shape[2]
    for h in range(cols_ref.shape[0]):
        for i in range(half // W):
            cols = cols_ref[h, :, i * W : (i + 1) * W]
            if h == 0 and i == 0:
                cols = cols + lt_ref[...].T * (place_ref[1] == 0).astype(jnp.float32)
            high, low = split(cols)
            at = slice(h * half + i * W, h * half + (i + 1) * W)
            for p, part in enumerate((high, low, high)):
                right_ref[p * W : (p + 1) * W, at] = part
    for i in range(rows_ref.shape[1] // W):
        at = slice(i * W, (i + 1) * W)
        rows = rows_ref[:, at].T
        if i == 0:
            rows = rows + lt_ref[...] * (place_ref[0] == 0).astype(jnp.float32)
        high, low = split(rows)
        both = jnp.concatenate([high, high, low], axis=1)
        reflect[at] = both
        out_ref[at, : 3 * W] = both
    t = tt_ref[...]
    mid = jnp.dot(t, inner_ref[...], precision=HIGHEST, preferred_element_type=jnp.float32)
    square = lax.dot_general(mid, t, (NT, ((), ())), precision=HIGHEST, preferred_element_type=jnp.float32)
    high, low = split(square)
    right = jnp.concatenate([high, low, high], axis=0)
    core = place_ref[1] % 2
    line = place_ref[1] // 2
    lines, part = own_ref.shape[:2]
    for s in range(lines):
        before = (line + lines - s) % lines
        for ref, k in ((own_ref, core), (other_ref, 1 - core)):
            at = pl.multiple_of((2 * before + k) * part, 16)
            weights = ref[s] - jnp.dot(reflect[pl.ds(at, part)], right, preferred_element_type=jnp.float32)
            high, low = split(weights)
            out_ref[pl.ds(at, part), 3 * W :] = jnp.concatenate([high, high, low], axis=1)


def prepare(place, panel_cols, panel_rows, own, other, factor_t, coupling_t, inner):
    rows = panel_rows.shape[1]
    cols = panel_cols.shape[0] * panel_cols.shape[2]
    vmem = pl.BlockSpec(memory_space=pltpu.VMEM)
    return pl.pallas_call(
        prepare_kernel,
        out_shape=[jax.ShapeDtypeStruct((rows, 6 * W), jnp.bfloat16), jax.ShapeDtypeStruct((3 * W, cols), jnp.bfloat16)],
        in_specs=[pl.BlockSpec(memory_space=pltpu.SMEM)] + [vmem] * 7,
        out_specs=[vmem] * 2,
        scratch_shapes=[pltpu.VMEM((rows, 3 * W), jnp.bfloat16)],
        compiler_params=pltpu.CompilerParams(vmem_limit_bytes=VMEM_BYTES),
        cost_estimate=pl.CostEstimate(flops=6 * rows * W * W, bytes_accessed=20 * rows * W, transcendentals=0),
    )(place, panel_cols, panel_rows, own, other, factor_t, coupling_t, inner)


def update_kernel(a_ref, left_ref, right_ref, weights_ref, out_ref):
    high, low = split(weights_ref[...].T)
    right = jnp.concatenate([high, low, high], axis=0)
    first = jnp.dot(left_ref[:, : 3 * W], right, preferred_element_type=jnp.float32)
    second = jnp.dot(left_ref[:, 3 * W :], right_ref[...], preferred_element_type=jnp.float32)
    out_ref[...] = a_ref[...] - (first + second)


def update(trailing, left, right, weight_cols):
    rows, cols = trailing.shape
    tile = 512
    return pl.pallas_call(
        update_kernel,
        grid=(cols // tile,),
        out_shape=jax.ShapeDtypeStruct((rows, cols), jnp.float32),
        in_specs=[
            pl.BlockSpec((rows, tile), lambda i: (0, i)),
            pl.BlockSpec((rows, 6 * W), lambda i: (0, 0)),
            pl.BlockSpec((3 * W, tile), lambda i: (0, i)),
            pl.BlockSpec((tile, W), lambda i: (i, 0)),
        ],
        out_specs=pl.BlockSpec((rows, tile), lambda i: (0, i)),
        compiler_params=pltpu.CompilerParams(vmem_limit_bytes=VMEM_BYTES),
        cost_estimate=pl.CostEstimate(flops=12 * rows * cols * W, bytes_accessed=8 * rows * cols, transcendentals=0),
    )(trailing, left, right, weight_cols)


def shards(trailing, panel_block):
    r = lax.axis_index("row")
    c = lax.axis_index("col")
    nr = lax.axis_size("row")
    nc = lax.axis_size("col")
    ratio = nr // nc
    perm = [(i * nc + j, ((i % ratio) * nc + j) * nc + i // ratio) for i in range(nr) for j in range(nc)]
    pair = [(j, j ^ 1) for j in range(nc)]
    lines = [list(range(k, nc, 2)) for k in range(2)]
    place = jnp.stack([r, c]).astype(jnp.int32)
    rows, width = panel_block.shape
    part = rows // nc
    panel_t = panel_block.T
    moved = lax.ppermute(panel_t, BOTH, perm)
    line = lax.all_gather(panel_t, "col", axis=0, axis_index_groups=lines)
    line, moved = lax.optimization_barrier((line, moved))
    other = lax.ppermute(line, "col", pair)
    even = c % 2 == 0
    panel_rows = jnp.stack([jnp.where(even, line, other), jnp.where(even, other, line)], axis=1).reshape(W, rows)
    panel_cols = lax.all_gather(moved, "row", axis=0, tiled=True).reshape(ratio, W, rows)
    strip = lax.dot_general(panel_t, panel_rows, (((1,), (1,)), ((), ())), precision=HIGHEST)
    top = jnp.where(r == 0, panel_t[:, :W], jnp.zeros((width, W), jnp.float32))
    pieces = to_tiles(jnp.concatenate([strip, top], axis=1))
    mine = jnp.sum(lax.all_to_all(pieces, "row", 0, 0, tiled=True), axis=0)
    full = lax.all_to_all(jnp.broadcast_to(mine[None], (nr * nc,) + mine.shape), BOTH, 0, 0, tiled=True)
    tr, tc = width // 8, 2 * W // H
    full = full.reshape(tr, tc, nc, 8, H).transpose(2, 0, 3, 1, 4).reshape(W, 2 * W)
    factor_t, coupling_t = factor(full[:, :W], full[:, W:].T)
    keep, send = product(place, trailing, panel_cols, panel_rows, factor_t, nc)
    pieces = keep + lax.ppermute(send, "col", pair)
    pieces = jnp.sum(lax.all_to_all(pieces, "col", 0, 0, tiled=True, axis_index_groups=lines), axis=0)
    mine, inner = pieces[:part], pieces[part:]
    mine = lax.dot_general(mine, coupling_t, (((1,), (1,)), ((), ())), precision=HIGHEST)
    moved = lax.ppermute(mine, BOTH, perm)
    weight_cols = lax.all_gather(moved, "row", axis=0, tiled=True)
    shifts = [[(j, (j + 2 * s) % nc) for j in range(nc)] for s in range(1, nc // 2)]
    line = jnp.stack([mine] + [lax.ppermute(mine, "col", shift) for shift in shifts])
    other = lax.ppermute(line, "col", pair)
    half = (nr, 8 * W * W // (8 * H * nr * nc), H)
    inner = jnp.sum(lax.all_to_all(to_tiles(inner).reshape(half), "row", 0, 0, tiled=True), axis=0)
    inner = jnp.broadcast_to(inner[None], (nr * nc,) + inner.shape)
    inner = lax.all_to_all(inner, BOTH, 0, 0, tiled=True).reshape((nr, nc) + inner.shape[1:])
    inner = from_tiles(inner.transpose(1, 0, 2, 3).reshape(-1, 8, H), W, W)
    left, right = prepare(place, panel_cols, panel_rows, line, other, factor_t, coupling_t, inner)
    return update(trailing, left, right, weight_cols)


def solution(mesh):
    return jax.shard_map(shards, mesh=mesh, in_specs=(P("row", "col"), P("row", "col")), out_specs=P("row", "col"), check_vma=False)
```

```python
import jax
import jax.numpy as jnp
from jax import lax
from jax.experimental import pallas as pl
from jax.experimental.pallas import tpu as pltpu
from jax.sharding import PartitionSpec as P

W = 256
H = 128
PANEL = 8
BOTH = ("row", "col")
HIGHEST = lax.Precision.HIGHEST


def lane(x, l):
    if x.shape[0] == 1:
        return lane(jnp.broadcast_to(x, (8, H)), l)[0:1]
    return jnp.take_along_axis(x, jnp.full(x.shape, l, jnp.int32), axis=1, mode="promise_in_bounds")


def panel_step(solo, rows, at):
    li = lax.broadcasted_iota(jnp.int32, (1, H), 1)
    sub = lax.broadcasted_iota(jnp.int32, (PANEL, H), 0)
    cols = [lane(rows, at + k) for k in range(PANEL)]
    mods, ratios, marks = [], [], []
    for a in range(PANEL):
        here = li == at + a
        row = rows[a : a + 1]
        tops = [cols[k][a : a + 1] for k in range(PANEL)]
        mod, ratio, final, mark = solo(a, here, row, tops)
        mods.append(mod)
        ratios.append(ratio)
        marks.append(mark)
        own = sub == a
        rows = jnp.where(own, final, rows - cols[a] * mod)
        for k in range(a + 1, PANEL):
            cols[k] = jnp.where(own, ratio[k], cols[k] - cols[a] * ratio[k])
    for a in range(PANEL - 2, -1, -1):
        for k in range(a + 1, PANEL):
            mods[a] = mods[a] - ratios[a][k] * mods[k]
    return rows, mods, marks


def update_rows(mat, cols, mods):
    new = mat[...]
    for col, mod in zip(cols, mods):
        new = new - col * mod
    mat[...] = new


def factor_kernel(gram_ref, top_ref, lt_ref, tt_ref, gw, vr, lt, lw, spread):
    ri = lax.broadcasted_iota(jnp.int32, (W, W), 0)
    ci = lax.broadcasted_iota(jnp.int32, (W, W), 1)
    li = lax.broadcasted_iota(jnp.int32, (1, H), 1)
    g = gram_ref[...]
    scale = 1.0 / jnp.max(jnp.where(ri == ci, g, 0.0), keepdims=True)
    root = jnp.sqrt(scale)
    t = top_ref[...] * root
    g = g * scale

    def dot(x, y):
        return jnp.dot(x, y, precision=HIGHEST, preferred_element_type=jnp.float32)

    def chol_panel(at):
        old = [lane(gw[...], at + k) for k in range(PANEL)]

        def solo(a, here, row, tops):
            d = tops[a]
            inv = 1.0 / d
            rs = lax.rsqrt(d)
            rs = rs * (1.5 - 0.5 * d * rs * rs)
            scaled = row * rs
            mod = jnp.where(here, 1.0 + inv, row * inv)
            ratio = [top * inv for top in tops]
            upper = jnp.where(li >= at + a, scaled, 0.0)
            lower = jnp.where(here, rs, jnp.where(li < at + a, scaled, 0.0))
            marks = [rs, scaled] + [top * rs for top in tops]
            return mod, ratio, row, (upper, lower, marks)

        _, mods, marks = panel_step(solo, gw[pl.ds(at, PANEL), :], at)
        update_rows(gw, old, mods)
        lt[pl.ds(at, PANEL), :] = jnp.concatenate([m[0] for m in marks], axis=0)
        lw[pl.ds(at, PANEL), :] = jnp.concatenate([m[1] for m in marks], axis=0)
        for a in range(PANEL):
            for i, x in enumerate(marks[a][2]):
                if i < 2 or i - 2 >= a:
                    spread[a, i : i + 1, :] = x

    def jordan_panel(at):
        old = [lane(vr[...], at + k) for k in range(PANEL)]
        marks = [[spread[a, i : i + 1, :] for i in range(PANEL + 2)] for a in range(PANEL)]

        def solo(a, here, row, tops):
            rs, scaled = marks[a][:2]
            row = row + scaled
            q = 1.0 / (tops[a] + marks[a][2 + a])
            norm = row * q
            rq = rs * q
            mod = jnp.where(here, 1.0 + rq, norm)
            final = jnp.where(here, rq, norm)
            ratio = [(tops[k] + marks[a][2 + k]) * q if k > a else None for k in range(PANEL)]
            return mod, ratio, final, None

        rows, mods, _ = panel_step(solo, vr[pl.ds(at, PANEL), :], at)
        update_rows(vr, old, mods)
        vr[pl.ds(at, PANEL), :] = rows

    def block(gram, top):
        gw[...] = gram
        vr[...] = top
        chol_panel(0)

        def body(i, _):
            at = pl.multiple_of(i * PANEL, PANEL)
            jordan_panel(at - PANEL)
            chol_panel(at)
            return 0

        lax.fori_loop(1, H // PANEL, body, 0)
        jordan_panel(H - PANEL)
        return lt[...], lw[...], vr[...]

    g12, g22 = g[:H, H:], g[H:, H:]
    l11t, w11, x11 = block(g[:H, :H], t[:H, :H])
    l21t = dot(w11, g12)
    l21 = l21t.T
    inv11 = dot(x11, l11t.T)
    v12 = t[:H, H:] + l21t
    k21 = dot(t[H:, :H], inv11)
    n12 = dot(inv11, v12)
    l22t, w22, x22 = block(g22 - dot(l21, l21t), t[H:, H:] - dot(k21, v12))
    t21 = -dot(x22, dot(l21 + dot(l22t.T, k21), w11))
    unroot = 1.0 / root
    lt_ref[:H, :H] = l11t * unroot
    lt_ref[:H, H:] = l21t * unroot
    lt_ref[H:, :H] = jnp.zeros((H, H), jnp.float32)
    lt_ref[H:, H:] = l22t * unroot
    tt_ref[:H, :H] = (x11 - dot(n12, t21)) * scale
    tt_ref[:H, H:] = -dot(n12, x22) * scale
    tt_ref[H:, :H] = t21 * scale
    tt_ref[H:, H:] = x22 * scale


def factor(gram, top):
    vmem = pl.BlockSpec(memory_space=pltpu.VMEM)
    return pl.pallas_call(
        factor_kernel,
        out_shape=[jax.ShapeDtypeStruct((W, W), jnp.float32)] * 2,
        in_specs=[vmem] * 2,
        out_specs=[vmem] * 2,
        scratch_shapes=[pltpu.VMEM((H, H), jnp.float32)] * 4 + [pltpu.VMEM((PANEL, PANEL + 2, H), jnp.float32)],
        cost_estimate=pl.CostEstimate(flops=2 * W**3, bytes_accessed=16 * W * W, transcendentals=0),
    )(gram, top)


def to_tiles(x):
    rows, cols = x.shape
    return x.reshape(rows // 8, 8, cols // H, H).transpose(0, 2, 1, 3).reshape(rows * cols // (8 * H), 8, H)


def split(x):
    high = x.astype(jnp.bfloat16)
    return high, (x - high.astype(jnp.float32)).astype(jnp.bfloat16)


NN = ((1,), (0,))
NT = ((1,), (1,))
VMEM_BYTES = 60 * 1024 * 1024


def dots(a, b, contract):
    a_high, a_low = split(a)
    b_high, b_low = split(b)
    left = jnp.concatenate([a_high, a_high, a_low], axis=contract[0][0])
    right = jnp.concatenate([b_high, b_low, b_high], axis=contract[1][0])
    return lax.dot_general(left, right, (contract, ((), ())), preferred_element_type=jnp.float32)


def product_kernel(place_ref, a_ref, cols_ref, rows_ref, lt_ref, keep_ref, send_ref, acc, inner_scr):
    step = pl.program_id(0)
    steps = pl.num_programs(0)

    @pl.when(step == 0)
    def _():
        own = (place_ref[1] == 0).astype(jnp.float32)
        cols = cols_ref[0]
        cols = jnp.concatenate([cols[:, :W] + own * lt_ref[...].T, cols[:, W:]], axis=1)
        acc[...] = dots(a_ref[...], cols, NT)

    @pl.when(step > 0)
    def _():
        acc[...] += dots(a_ref[...], cols_ref[0], NT)

    @pl.when(step == steps - 1)
    def _():
        own = (place_ref[0] == 0).astype(jnp.float32)
        inner = dots(rows_ref[:, :W] + own * lt_ref[...].T, acc[:W], NN)
        inner = inner + dots(rows_ref[:, W:], acc[W:], NN)
        inner_scr[...] = inner
        lines = keep_ref.shape[0]
        part = acc.shape[0] // (2 * lines)
        size = W // (2 * lines)
        line = place_ref[1] // 2
        core = place_ref[1] % 2
        for q in range(lines):
            for target, k in ((keep_ref, core), (send_ref, 1 - core)):
                i = 2 * ((line + q) % lines) + k
                target[q, :part] = acc[pl.ds(pl.multiple_of(i * part, 8), part)]
                target[q, part:] = inner_scr[pl.ds(pl.multiple_of(i * size, 8), size)]


def product(place, trailing, panel_cols, panel_rows, factor_t, parts):
    rows, cols = trailing.shape
    half = panel_cols.shape[2]
    tile = 640
    per = half // tile
    out = jax.ShapeDtypeStruct((parts // 2, (rows + W) // parts, W), jnp.float32)
    out_spec = pl.BlockSpec(out.shape, lambda i: (0, 0, 0))
    return pl.pallas_call(
        product_kernel,
        grid=(cols // tile,),
        out_shape=[out, out],
        in_specs=[
            pl.BlockSpec(memory_space=pltpu.SMEM),
            pl.BlockSpec((rows, tile), lambda i: (0, i)),
            pl.BlockSpec((1, W, tile), lambda i: (i // per, 0, i % per)),
            pl.BlockSpec((W, rows), lambda i: (0, 0)),
            pl.BlockSpec((W, W), lambda i: (0, 0)),
        ],
        out_specs=[out_spec, out_spec],
        scratch_shapes=[pltpu.VMEM((rows, W), jnp.float32), pltpu.VMEM((W, W), jnp.float32)],
        compiler_params=pltpu.CompilerParams(vmem_limit_bytes=VMEM_BYTES),
        cost_estimate=pl.CostEstimate(flops=6 * rows * cols * W, bytes_accessed=4 * rows * cols, transcendentals=0),
    )(place, trailing, panel_cols, panel_rows, factor_t)


def prepare_kernel(place_ref, cols_ref, rows_ref, own_ref, other_ref, lt_ref, tt_ref, inner_ref, out_ref, right_ref, reflect):
    half = cols_ref.shape[2]
    for h in range(cols_ref.shape[0]):
        for i in range(half // W):
            cols = cols_ref[h, :, i * W : (i + 1) * W]
            if h == 0 and i == 0:
                cols = cols + lt_ref[...].T * (place_ref[1] == 0).astype(jnp.float32)
            high, low = split(cols)
            at = slice(h * half + i * W, h * half + (i + 1) * W)
            for p, part in enumerate((high, low, high)):
                right_ref[p * W : (p + 1) * W, at] = part
    for i in range(rows_ref.shape[1] // W):
        at = slice(i * W, (i + 1) * W)
        rows = rows_ref[:, at].T
        if i == 0:
            rows = rows + lt_ref[...] * (place_ref[0] == 0).astype(jnp.float32)
        high, low = split(rows)
        both = jnp.concatenate([high, high, low], axis=1)
        reflect[at] = both
        out_ref[at, : 3 * W] = both
    t = tt_ref[...]
    mid = jnp.dot(t, inner_ref[...], precision=HIGHEST, preferred_element_type=jnp.float32)
    square = lax.dot_general(mid, t, (NT, ((), ())), precision=HIGHEST, preferred_element_type=jnp.float32)
    high, low = split(square)
    right = jnp.concatenate([high, low, high], axis=0)
    core = place_ref[1] % 2
    line = place_ref[1] // 2
    lines, part = own_ref.shape[:2]
    for s in range(lines):
        before = (line + lines - s) % lines
        for ref, k in ((own_ref, core), (other_ref, 1 - core)):
            at = pl.multiple_of((2 * before + k) * part, 16)
            weights = ref[s] - jnp.dot(reflect[pl.ds(at, part)], right, preferred_element_type=jnp.float32)
            high, low = split(weights)
            out_ref[pl.ds(at, part), 3 * W :] = jnp.concatenate([high, high, low], axis=1)


def prepare(place, panel_cols, panel_rows, own, other, factor_t, coupling_t, inner):
    rows = panel_rows.shape[1]
    cols = panel_cols.shape[0] * panel_cols.shape[2]
    vmem = pl.BlockSpec(memory_space=pltpu.VMEM)
    return pl.pallas_call(
        prepare_kernel,
        out_shape=[jax.ShapeDtypeStruct((rows, 6 * W), jnp.bfloat16), jax.ShapeDtypeStruct((3 * W, cols), jnp.bfloat16)],
        in_specs=[pl.BlockSpec(memory_space=pltpu.SMEM)] + [vmem] * 7,
        out_specs=[vmem] * 2,
        scratch_shapes=[pltpu.VMEM((rows, 3 * W), jnp.bfloat16)],
        compiler_params=pltpu.CompilerParams(vmem_limit_bytes=VMEM_BYTES),
        cost_estimate=pl.CostEstimate(flops=6 * rows * W * W, bytes_accessed=20 * rows * W, transcendentals=0),
    )(place, panel_cols, panel_rows, own, other, factor_t, coupling_t, inner)


def update_kernel(a_ref, left_ref, right_ref, weights_ref, out_ref):
    high, low = split(weights_ref[...].T)
    right = jnp.concatenate([high, low, high], axis=0)
    first = jnp.dot(left_ref[:, : 3 * W], right, preferred_element_type=jnp.float32)
    second = jnp.dot(left_ref[:, 3 * W :], right_ref[...], preferred_element_type=jnp.float32)
    out_ref[...] = a_ref[...] - (first + second)


def update(trailing, left, right, weight_cols):
    rows, cols = trailing.shape
    tile = 512
    return pl.pallas_call(
        update_kernel,
        grid=(cols // tile,),
        out_shape=jax.ShapeDtypeStruct((rows, cols), jnp.float32),
        in_specs=[
            pl.BlockSpec((rows, tile), lambda i: (0, i)),
            pl.BlockSpec((rows, 6 * W), lambda i: (0, 0)),
            pl.BlockSpec((3 * W, tile), lambda i: (0, i)),
            pl.BlockSpec((tile, W), lambda i: (i, 0)),
        ],
        out_specs=pl.BlockSpec((rows, tile), lambda i: (0, i)),
        compiler_params=pltpu.CompilerParams(vmem_limit_bytes=VMEM_BYTES),
        cost_estimate=pl.CostEstimate(flops=12 * rows * cols * W, bytes_accessed=8 * rows * cols, transcendentals=0),
    )(trailing, left, right, weight_cols)


def shards(trailing, panel_block):
    r = lax.axis_index("row")
    c = lax.axis_index("col")
    nr = lax.axis_size("row")
    nc = lax.axis_size("col")
    ratio = nr // nc

    def home(i, j):
        return ((i % ratio) * nc + j) * nc + i // ratio

    def after(j, s):
        return (j + 2 * s) % nc

    perm = [(i * nc + j, home(i, j)) for i in range(nr) for j in range(nc)]
    pair = [(j, j ^ 1) for j in range(nc)]
    lines = [list(range(k, nc, 2)) for k in range(2)]
    place = jnp.stack([r, c]).astype(jnp.int32)
    rows, width = panel_block.shape
    part = rows // nc
    panel_t = panel_block.T
    moved = lax.ppermute(panel_t, BOTH, perm)
    line = lax.all_gather(panel_t, "col", axis=0, axis_index_groups=lines)
    line, moved = lax.optimization_barrier((line, moved))
    other = lax.ppermute(line, "col", pair)
    even = c % 2 == 0
    panel_rows = jnp.stack([jnp.where(even, line, other), jnp.where(even, other, line)], axis=1).reshape(W, rows)
    panel_cols = lax.all_gather(moved, "row", axis=0, tiled=True).reshape(ratio, W, rows)
    strip = lax.dot_general(panel_t, panel_rows, (((1,), (1,)), ((), ())), precision=HIGHEST)
    top = jnp.where(r == 0, panel_t[:, :W], jnp.zeros((width, W), jnp.float32))
    pieces = to_tiles(jnp.concatenate([strip, top], axis=1))
    mine = jnp.sum(lax.all_to_all(pieces, "row", 0, 0, tiled=True), axis=0)
    full = lax.all_to_all(jnp.broadcast_to(mine[None], (nr * nc,) + mine.shape), BOTH, 0, 0, tiled=True)
    tr, tc = width // 8, 2 * W // H
    full = full.reshape(tr, tc, nc, 8, H).transpose(2, 0, 3, 1, 4).reshape(W, 2 * W)
    factor_t, coupling_t = factor(full[:, :W], full[:, W:].T)
    keep, send = product(place, trailing, panel_cols, panel_rows, factor_t, nc)
    pieces = keep + lax.ppermute(send, "col", pair)
    out = [[(i * nc + j, home(i, after(j, s))) for i in range(nr) for j in range(nc)] for s in range(nc // 2)]
    back = [[(home(i, j), i * nc + after(j, s)) for i in range(nr) for j in range(nc)] for s in range(nc // 2)]
    pieces = sum(lax.ppermute(pieces[s], BOTH, out[s]) for s in range(nc // 2))
    mine, inner = pieces[:part], pieces[part:]
    mine = lax.dot_general(mine, coupling_t, (((1,), (1,)), ((), ())), precision=HIGHEST)
    weight_cols = lax.all_gather(mine, "row", axis=0, tiled=True)
    line = jnp.stack([lax.ppermute(mine, BOTH, back[s]) for s in range(nc // 2)])
    other = lax.ppermute(line, "col", pair)
    groups = [[home(i, j) for i in range(nr)] for j in range(nc)]
    inner = jnp.broadcast_to(inner[None], (nr,) + inner.shape)
    inner = jnp.sum(lax.all_to_all(inner, BOTH, 0, 0, tiled=True, axis_index_groups=groups), axis=0)
    inner = jnp.broadcast_to(inner[None], (nc,) + inner.shape)
    strips = [list(range(h * nc, (h + 1) * nc)) for h in range(ratio)]
    inner = lax.all_to_all(inner, "row", 0, 0, tiled=True, axis_index_groups=strips).reshape(W, W)
    left, right = prepare(place, panel_cols, panel_rows, line, other, factor_t, coupling_t, inner)
    return update(trailing, left, right, weight_cols)


def solution(mesh):
    return jax.shard_map(shards, mesh=mesh, in_specs=(P("row", "col"), P("row", "col")), out_specs=P("row", "col"), check_vma=False)
```

```python
import jax
import jax.numpy as jnp
from jax import lax
from jax.experimental import pallas as pl
from jax.experimental.pallas import tpu as pltpu
from jax.sharding import PartitionSpec as P

W = 256
H = 128
PANEL = 8
STRIPS = 8
BOTH = ("row", "col")
HIGHEST = lax.Precision.HIGHEST


def lane(x, l):
    if x.shape[0] == 1:
        return lane(jnp.broadcast_to(x, (8, H)), l)[0:1]
    return jnp.take_along_axis(x, jnp.full(x.shape, l, jnp.int32), axis=1, mode="promise_in_bounds")


def panel_step(solo, rows, at):
    li = lax.broadcasted_iota(jnp.int32, (1, H), 1)
    sub = lax.broadcasted_iota(jnp.int32, (PANEL, H), 0)
    cols = [lane(rows, at + k) for k in range(PANEL)]
    mods, ratios, marks = [], [], []
    for a in range(PANEL):
        here = li == at + a
        row = rows[a : a + 1]
        tops = [cols[k][a : a + 1] for k in range(PANEL)]
        mod, ratio, final, mark = solo(a, here, row, tops)
        mods.append(mod)
        ratios.append(ratio)
        marks.append(mark)
        own = sub == a
        rows = jnp.where(own, final, rows - cols[a] * mod)
        for k in range(a + 1, PANEL):
            cols[k] = jnp.where(own, ratio[k], cols[k] - cols[a] * ratio[k])
    for a in range(PANEL - 2, -1, -1):
        for k in range(a + 1, PANEL):
            mods[a] = mods[a] - ratios[a][k] * mods[k]
    return rows, mods, marks


def update_rows(mat, first, cols, mods):
    new = mat[first:]
    for col, mod in zip(cols, mods):
        new = new - col * mod
    mat[first:] = new


def factor_kernel(pieces_ref, lt_ref, tt_ref, gw, vr, lt, lw, spread, whole):
    ri = lax.broadcasted_iota(jnp.int32, (W, W), 0)
    ci = lax.broadcasted_iota(jnp.int32, (W, W), 1)
    li = lax.broadcasted_iota(jnp.int32, (1, H), 1)
    across = 2 * W // H
    strip = W // STRIPS
    tiles = strip // 8 * across
    for t in range(tiles):
        for c in range(STRIPS):
            row = c * strip + t // across * 8
            whole[row : row + 8, t % across * H : (t % across + 1) * H] = pieces_ref[t * STRIPS + c]
    g = whole[:, :W]
    scale = 1.0 / jnp.max(jnp.where(ri == ci, g, 0.0), keepdims=True)
    root = jnp.sqrt(scale)
    t = whole[:, W:].T * root
    g = g * scale

    def dot(x, y):
        return jnp.dot(x, y, precision=HIGHEST, preferred_element_type=jnp.float32)

    def chol_panel(at, first):
        old = [lane(gw[first:], at + k) for k in range(PANEL)]

        def solo(a, here, row, tops):
            d = tops[a]
            inv = 1.0 / d
            rs = lax.rsqrt(d)
            rs = rs * (1.5 - 0.5 * d * rs * rs)
            scaled = row * rs
            mod = jnp.where(here, 1.0 + inv, row * inv)
            ratio = [top * inv for top in tops]
            upper = jnp.where(li >= at + a, scaled, 0.0)
            lower = jnp.where(here, rs, jnp.where(li < at + a, scaled, 0.0))
            marks = [rs, scaled] + [top * rs for top in tops]
            return mod, ratio, row, (upper, lower, marks)

        _, mods, marks = panel_step(solo, gw[pl.ds(at, PANEL), :], at)
        update_rows(gw, first, old, mods)
        lt[pl.ds(at, PANEL), :] = jnp.concatenate([m[0] for m in marks], axis=0)
        lw[pl.ds(at, PANEL), :] = jnp.concatenate([m[1] for m in marks], axis=0)
        for a in range(PANEL):
            for i, x in enumerate(marks[a][2]):
                if i < 2 or i - 2 >= a:
                    spread[a, i : i + 1, :] = x

    def jordan_panel(at):
        old = [lane(vr[...], at + k) for k in range(PANEL)]
        marks = [[spread[a, i : i + 1, :] for i in range(PANEL + 2)] for a in range(PANEL)]

        def solo(a, here, row, tops):
            rs, scaled = marks[a][:2]
            row = row + scaled
            q = 1.0 / (tops[a] + marks[a][2 + a])
            norm = row * q
            rq = rs * q
            mod = jnp.where(here, 1.0 + rq, norm)
            final = jnp.where(here, rq, norm)
            ratio = [(tops[k] + marks[a][2 + k]) * q if k > a else None for k in range(PANEL)]
            return mod, ratio, final, None

        rows, mods, _ = panel_step(solo, vr[pl.ds(at, PANEL), :], at)
        update_rows(vr, 0, old, mods)
        vr[pl.ds(at, PANEL), :] = rows

    def block(gram, top):
        gw[...] = gram
        vr[...] = top
        chol_panel(0, 0)
        for first in range(0, H, H // 4):

            def body(i, _, first=first):
                at = pl.multiple_of(i * PANEL, PANEL)
                jordan_panel(at - PANEL)
                chol_panel(at, first)
                return 0

            lax.fori_loop(max(first // PANEL, 1), (first + H // 4) // PANEL, body, 0)
        jordan_panel(H - PANEL)
        return lt[...], lw[...], vr[...]

    g12, g22 = g[:H, H:], g[H:, H:]
    l11t, w11, x11 = block(g[:H, :H], t[:H, :H])
    l21t = dot(w11, g12)
    l21 = l21t.T
    inv11 = dot(x11, l11t.T)
    v12 = t[:H, H:] + l21t
    k21 = dot(t[H:, :H], inv11)
    n12 = dot(inv11, v12)
    l22t, w22, x22 = block(g22 - dot(l21, l21t), t[H:, H:] - dot(k21, v12))
    t21 = -dot(x22, dot(l21 + dot(l22t.T, k21), w11))
    unroot = 1.0 / root
    lt_ref[:H, :H] = l11t * unroot
    lt_ref[:H, H:] = l21t * unroot
    lt_ref[H:, :H] = jnp.zeros((H, H), jnp.float32)
    lt_ref[H:, H:] = l22t * unroot
    tt_ref[:H, :H] = (x11 - dot(n12, t21)) * scale
    tt_ref[:H, H:] = -dot(n12, x22) * scale
    tt_ref[H:, :H] = t21 * scale
    tt_ref[H:, H:] = x22 * scale


def factor(pieces):
    vmem = pl.BlockSpec(memory_space=pltpu.VMEM)
    square = pltpu.VMEM((H, H), jnp.float32)
    return pl.pallas_call(
        factor_kernel,
        out_shape=[jax.ShapeDtypeStruct((W, W), jnp.float32)] * 2,
        in_specs=[vmem],
        out_specs=[vmem] * 2,
        scratch_shapes=[square] * 4 + [pltpu.VMEM((PANEL, PANEL + 2, H), jnp.float32), pltpu.VMEM((W, 2 * W), jnp.float32)],
        cost_estimate=pl.CostEstimate(flops=2 * W**3, bytes_accessed=16 * W * W, transcendentals=0),
    )(pieces)


def to_tiles(x):
    rows, cols = x.shape
    return x.reshape(rows // 8, 8, cols // H, H).transpose(0, 2, 1, 3).reshape(rows * cols // (8 * H), 8, H)


def from_tiles(x, rows, cols):
    return x.reshape(rows // 8, cols // H, 8, H).transpose(0, 2, 1, 3).reshape(rows, cols)


def split(x):
    high = x.astype(jnp.bfloat16)
    return high, (x - high.astype(jnp.float32)).astype(jnp.bfloat16)


NN = ((1,), (0,))
NT = ((1,), (1,))
VMEM_BYTES = 60 * 1024 * 1024


def dots(a, b, contract):
    a_high, a_low = split(a)
    b_high, b_low = split(b)
    left = jnp.concatenate([a_high, a_high, a_low], axis=contract[0][0])
    right = jnp.concatenate([b_high, b_low, b_high], axis=contract[1][0])
    return lax.dot_general(left, right, (contract, ((), ())), preferred_element_type=jnp.float32)


def product_kernel(place_ref, a_ref, cols_ref, rows_ref, lt_ref, keep_ref, send_ref, acc, inner_scr):
    step = pl.program_id(0)
    steps = pl.num_programs(0)

    @pl.when(step == 0)
    def _():
        own = (place_ref[1] == 0).astype(jnp.float32)
        cols = cols_ref[0]
        cols = jnp.concatenate([cols[:, :W] + own * lt_ref[...].T, cols[:, W:]], axis=1)
        acc[...] = dots(a_ref[...], cols, NT)

    @pl.when(step > 0)
    def _():
        acc[...] += dots(a_ref[...], cols_ref[0], NT)

    @pl.when(step == steps - 1)
    def _():
        own = (place_ref[0] == 0).astype(jnp.float32)
        inner = dots(rows_ref[:, :W] + own * lt_ref[...].T, acc[:W], NN)
        inner = inner + dots(rows_ref[:, W:], acc[W:], NN)
        inner_scr[...] = inner
        lines = keep_ref.shape[0]
        part = acc.shape[0] // (2 * lines)
        size = W // (2 * lines)
        line = place_ref[1] // 2
        core = place_ref[1] % 2
        for q in range(lines):
            for target, k in ((keep_ref, core), (send_ref, 1 - core)):
                i = 2 * ((line + q) % lines) + k
                target[q, :part] = acc[pl.ds(pl.multiple_of(i * part, 8), part)]
                target[q, part:] = inner_scr[pl.ds(pl.multiple_of(i * size, 8), size)]


def product(place, trailing, panel_cols, panel_rows, factor_t, parts):
    rows, cols = trailing.shape
    half = panel_cols.shape[2]
    tile = 640
    per = half // tile
    out = jax.ShapeDtypeStruct((parts // 2, (rows + W) // parts, W), jnp.float32)
    out_spec = pl.BlockSpec(out.shape, lambda i: (0, 0, 0))
    return pl.pallas_call(
        product_kernel,
        grid=(cols // tile,),
        out_shape=[out, out],
        in_specs=[
            pl.BlockSpec(memory_space=pltpu.SMEM),
            pl.BlockSpec((rows, tile), lambda i: (0, i)),
            pl.BlockSpec((1, W, tile), lambda i: (i // per, 0, i % per)),
            pl.BlockSpec((W, rows), lambda i: (0, 0)),
            pl.BlockSpec((W, W), lambda i: (0, 0)),
        ],
        out_specs=[out_spec, out_spec],
        scratch_shapes=[pltpu.VMEM((rows, W), jnp.float32), pltpu.VMEM((W, W), jnp.float32)],
        compiler_params=pltpu.CompilerParams(vmem_limit_bytes=VMEM_BYTES),
        cost_estimate=pl.CostEstimate(flops=6 * rows * cols * W, bytes_accessed=4 * rows * cols, transcendentals=0),
    )(place, trailing, panel_cols, panel_rows, factor_t)


def parts_kernel(place_ref, cols_ref, rows_ref, lt_ref, left_ref, right_ref):
    half = cols_ref.shape[2]
    lt = lt_ref[...]
    for i in range(rows_ref.shape[1] // W):
        at = slice(i * W, (i + 1) * W)
        rows = rows_ref[:, at].T
        if i == 0:
            rows = rows + lt * (place_ref[0] == 0).astype(jnp.float32)
        high, low = split(rows)
        for p, part in enumerate((high, high, low)):
            left_ref[at, p * W : (p + 1) * W] = part
    for h in range(cols_ref.shape[0]):
        for i in range(half // W):
            cols = cols_ref[h, :, i * W : (i + 1) * W]
            if h == 0 and i == 0:
                cols = cols + lt.T * (place_ref[1] == 0).astype(jnp.float32)
            high, low = split(cols)
            at = slice(h * half + i * W, h * half + (i + 1) * W)
            for p, part in enumerate((high, low, high)):
                right_ref[p * W : (p + 1) * W, at] = part


def parts_of(place, panel_cols, panel_rows, factor_t):
    rows = panel_rows.shape[1]
    cols = panel_cols.shape[0] * panel_cols.shape[2]
    vmem = pl.BlockSpec(memory_space=pltpu.VMEM)
    return pl.pallas_call(
        parts_kernel,
        out_shape=[jax.ShapeDtypeStruct(shape, jnp.bfloat16) for shape in ((rows, 3 * W), (3 * W, cols))],
        in_specs=[pl.BlockSpec(memory_space=pltpu.SMEM)] + [vmem] * 3,
        out_specs=[vmem] * 2,
        compiler_params=pltpu.CompilerParams(vmem_limit_bytes=VMEM_BYTES),
        cost_estimate=pl.CostEstimate(flops=8 * rows * W, bytes_accessed=10 * (rows + cols) * W, transcendentals=0),
    )(place, panel_cols, panel_rows, factor_t)


def correct_kernel(place_ref, left_ref, own_ref, other_ref, tt_ref, inner_ref, out_ref):
    t = tt_ref[...]
    mid = jnp.dot(t, inner_ref[...], precision=HIGHEST, preferred_element_type=jnp.float32)
    square = lax.dot_general(mid, t, (NT, ((), ())), precision=HIGHEST, preferred_element_type=jnp.float32)
    high, low = split(square)
    right = jnp.concatenate([high, low, high], axis=0)
    core = place_ref[1] % 2
    line = place_ref[1] // 2
    lines, part = own_ref.shape[:2]
    for s in range(lines):
        before = (line + lines - s) % lines
        for ref, k in ((own_ref, core), (other_ref, 1 - core)):
            at = pl.multiple_of((2 * before + k) * part, 16)
            weights = ref[s] - jnp.dot(left_ref[pl.ds(at, part)], right, preferred_element_type=jnp.float32)
            high, low = split(weights)
            out_ref[pl.ds(at, part)] = jnp.concatenate([high, high, low], axis=1)


def correct(place, left, own, other, coupling_t, inner):
    vmem = pl.BlockSpec(memory_space=pltpu.VMEM)
    return pl.pallas_call(
        correct_kernel,
        out_shape=jax.ShapeDtypeStruct(left.shape, jnp.bfloat16),
        in_specs=[pl.BlockSpec(memory_space=pltpu.SMEM)] + [vmem] * 5,
        out_specs=vmem,
        compiler_params=pltpu.CompilerParams(vmem_limit_bytes=VMEM_BYTES),
        cost_estimate=pl.CostEstimate(flops=2 * left.size * W, bytes_accessed=8 * left.size, transcendentals=0),
    )(place, left, own, other, coupling_t, inner)


def update_kernel(a_ref, left_ref, wleft_ref, right_ref, weights_ref, out_ref):
    high, low = split(weights_ref[...].T)
    right = jnp.concatenate([high, low, high], axis=0)
    first = jnp.dot(left_ref[...], right, preferred_element_type=jnp.float32)
    second = jnp.dot(wleft_ref[...], right_ref[...], preferred_element_type=jnp.float32)
    out_ref[...] = a_ref[...] - (first + second)


def update(trailing, left, weight_left, right, weight_cols):
    rows, cols = trailing.shape
    tile = 512
    return pl.pallas_call(
        update_kernel,
        grid=(cols // tile,),
        out_shape=jax.ShapeDtypeStruct((rows, cols), jnp.float32),
        in_specs=[
            pl.BlockSpec((rows, tile), lambda i: (0, i)),
            pl.BlockSpec((rows, 3 * W), lambda i: (0, 0)),
            pl.BlockSpec((rows, 3 * W), lambda i: (0, 0)),
            pl.BlockSpec((3 * W, tile), lambda i: (0, i)),
            pl.BlockSpec((tile, W), lambda i: (i, 0)),
        ],
        out_specs=pl.BlockSpec((rows, tile), lambda i: (0, i)),
        compiler_params=pltpu.CompilerParams(vmem_limit_bytes=VMEM_BYTES),
        cost_estimate=pl.CostEstimate(flops=12 * rows * cols * W, bytes_accessed=8 * rows * cols, transcendentals=0),
    )(trailing, left, weight_left, right, weight_cols)


def shards(trailing, panel_block):
    r = lax.axis_index("row")
    c = lax.axis_index("col")
    nr = lax.axis_size("row")
    nc = lax.axis_size("col")
    ratio = nr // nc
    perm = [(i * nc + j, ((i % ratio) * nc + j) * nc + i // ratio) for i in range(nr) for j in range(nc)]
    pair = [(j, j ^ 1) for j in range(nc)]
    lines = [list(range(k, nc, 2)) for k in range(2)]
    place = jnp.stack([r, c]).astype(jnp.int32)
    rows, width = panel_block.shape
    part = rows // nc
    panel_t = panel_block.T
    moved = lax.ppermute(panel_t, BOTH, perm)
    line = lax.all_gather(panel_t, "col", axis=0, axis_index_groups=lines)
    line, moved = lax.optimization_barrier((line, moved))
    other = lax.ppermute(line, "col", pair)
    even = c % 2 == 0
    panel_rows = jnp.stack([jnp.where(even, line, other), jnp.where(even, other, line)], axis=1).reshape(W, rows)
    panel_cols = lax.all_gather(moved, "row", axis=0, tiled=True).reshape(ratio, W, rows)
    strip = lax.dot_general(panel_t, panel_rows, (((1,), (1,)), ((), ())), precision=HIGHEST)
    top = jnp.where(r == 0, panel_t[:, :W], jnp.zeros((width, W), jnp.float32))
    pieces = to_tiles(jnp.concatenate([strip, top], axis=1))
    mine = jnp.sum(lax.all_to_all(pieces, "row", 0, 0, tiled=True), axis=0)
    full = lax.all_to_all(jnp.broadcast_to(mine[None], (nr * nc,) + mine.shape), BOTH, 0, 0, tiled=True)
    factor_t, coupling_t = factor(full)
    keep, send = product(place, trailing, panel_cols, panel_rows, factor_t, nc)
    pieces = keep + lax.ppermute(send, "col", pair)
    shifts = [[(j, (j + 2 * s) % nc) for j in range(nc)] for s in range(1, nc // 2)]
    pieces = pieces[0] + sum(lax.ppermute(pieces[s + 1], "col", shift) for s, shift in enumerate(shifts))
    mine, inner = pieces[:part], pieces[part:]
    mine = lax.dot_general(mine, coupling_t, (((1,), (1,)), ((), ())), precision=HIGHEST)
    mine, later = lax.optimization_barrier((mine, panel_rows))
    moved = lax.ppermute(mine, BOTH, perm)
    left, right = parts_of(place, panel_cols, later, factor_t)
    moved, left = lax.optimization_barrier((moved, left))
    weight_cols = lax.all_gather(moved, "row", axis=0, tiled=True)
    line = jnp.stack([mine] + [lax.ppermute(mine, "col", shift) for shift in shifts])
    half = (nr, 8 * W * W // (8 * H * nr * nc), H)
    inner = jnp.sum(lax.all_to_all(to_tiles(inner).reshape(half), "row", 0, 0, tiled=True), axis=0)
    line, inner = lax.optimization_barrier((line, inner))
    other = lax.ppermute(line, "col", pair)
    inner = jnp.broadcast_to(inner[None], (nr * nc,) + inner.shape)
    inner = lax.all_to_all(inner, BOTH, 0, 0, tiled=True).reshape((nr, nc) + inner.shape[1:])
    inner = from_tiles(inner.transpose(1, 0, 2, 3).reshape(-1, 8, H), W, W)
    weight_left = correct(place, left, line, other, coupling_t, inner)
    return update(trailing, left, weight_left, right, weight_cols)


def solution(mesh):
    return jax.shard_map(shards, mesh=mesh, in_specs=(P("row", "col"), P("row", "col")), out_specs=P("row", "col"), check_vma=False)
```

```python
import jax
import jax.numpy as jnp
from jax import lax
from jax.experimental import pallas as pl
from jax.experimental.pallas import tpu as pltpu
from jax.sharding import PartitionSpec as P

W = 256
H = 128
PANEL = 8
STRIPS = 8
BOTH = ("row", "col")
HIGHEST = lax.Precision.HIGHEST


def lane(x, l):
    if x.shape[0] == 1:
        return lane(jnp.broadcast_to(x, (8, H)), l)[0:1]
    return jnp.take_along_axis(x, jnp.full(x.shape, l, jnp.int32), axis=1, mode="promise_in_bounds")


def panel_step(solo, rows, at):
    li = lax.broadcasted_iota(jnp.int32, (1, H), 1)
    sub = lax.broadcasted_iota(jnp.int32, (PANEL, H), 0)
    cols = [lane(rows, at + k) for k in range(PANEL)]
    mods, ratios, marks = [], [], []
    for a in range(PANEL):
        here = li == at + a
        row = rows[a : a + 1]
        tops = [cols[k][a : a + 1] for k in range(PANEL)]
        mod, ratio, final, mark = solo(a, here, row, tops)
        mods.append(mod)
        ratios.append(ratio)
        marks.append(mark)
        own = sub == a
        rows = jnp.where(own, final, rows - cols[a] * mod)
        for k in range(a + 1, PANEL):
            cols[k] = jnp.where(own, ratio[k], cols[k] - cols[a] * ratio[k])
    for a in range(PANEL - 2, -1, -1):
        for k in range(a + 1, PANEL):
            mods[a] = mods[a] - ratios[a][k] * mods[k]
    return rows, mods, marks


def update_rows(mat, first, cols, mods):
    new = mat[first:]
    for col, mod in zip(cols, mods):
        new = new - col * mod
    mat[first:] = new


def factor_kernel(pieces_ref, lt_ref, tt_ref, gw, vr, lt, lw, spread, whole):
    ri = lax.broadcasted_iota(jnp.int32, (W, W), 0)
    ci = lax.broadcasted_iota(jnp.int32, (W, W), 1)
    li = lax.broadcasted_iota(jnp.int32, (1, H), 1)
    across = 2 * W // H
    strip = W // STRIPS
    tiles = strip // 8 * across
    for t in range(tiles):
        for c in range(STRIPS):
            row = c * strip + t // across * 8
            whole[row : row + 8, t % across * H : (t % across + 1) * H] = pieces_ref[t * STRIPS + c]
    g = whole[:, :W]
    scale = 1.0 / jnp.max(jnp.where(ri == ci, g, 0.0), keepdims=True)
    root = jnp.sqrt(scale)
    t = whole[:, W:].T * root
    g = g * scale

    def dot(x, y):
        return jnp.dot(x, y, precision=HIGHEST, preferred_element_type=jnp.float32)

    def chol_panel(at):
        old = [lane(gw[at:], at + k) for k in range(PANEL)]

        def solo(a, here, row, tops):
            d = tops[a]
            inv = 1.0 / d
            rs = lax.rsqrt(d)
            rs = rs * (1.5 - 0.5 * d * rs * rs)
            scaled = row * rs
            mod = jnp.where(here, 1.0 + inv, row * inv)
            ratio = [top * inv for top in tops]
            upper = jnp.where(li >= at + a, scaled, 0.0)
            lower = jnp.where(here, rs, jnp.where(li < at + a, scaled, 0.0))
            marks = [rs, scaled] + [top * rs for top in tops]
            return mod, ratio, row, (upper, lower, marks)

        _, mods, marks = panel_step(solo, gw[pl.ds(at, PANEL), :], at)
        update_rows(gw, at, old, mods)
        lt[pl.ds(at, PANEL), :] = jnp.concatenate([m[0] for m in marks], axis=0)
        lw[pl.ds(at, PANEL), :] = jnp.concatenate([m[1] for m in marks], axis=0)
        for a in range(PANEL):
            for i, x in enumerate(marks[a][2]):
                if i < 2 or i - 2 >= a:
                    spread[a, i : i + 1, :] = x

    def jordan_panel(at):
        old = [lane(vr[...], at + k) for k in range(PANEL)]
        marks = [[spread[a, i : i + 1, :] for i in range(PANEL + 2)] for a in range(PANEL)]

        def solo(a, here, row, tops):
            rs, scaled = marks[a][:2]
            row = row + scaled
            q = 1.0 / (tops[a] + marks[a][2 + a])
            norm = row * q
            rq = rs * q
            mod = jnp.where(here, 1.0 + rq, norm)
            final = jnp.where(here, rq, norm)
            ratio = [(tops[k] + marks[a][2 + k]) * q if k > a else None for k in range(PANEL)]
            return mod, ratio, final, None

        rows, mods, _ = panel_step(solo, vr[pl.ds(at, PANEL), :], at)
        update_rows(vr, 0, old, mods)
        vr[pl.ds(at, PANEL), :] = rows

    def block(gram, top):
        gw[...] = gram
        vr[...] = top
        chol_panel(0)
        for at in range(PANEL, H, PANEL):
            jordan_panel(at - PANEL)
            chol_panel(at)
        jordan_panel(H - PANEL)
        return lt[...], lw[...], vr[...]

    g12, g22 = g[:H, H:], g[H:, H:]
    l11t, w11, x11 = block(g[:H, :H], t[:H, :H])
    l21t = dot(w11, g12)
    l21 = l21t.T
    inv11 = dot(x11, l11t.T)
    v12 = t[:H, H:] + l21t
    k21 = dot(t[H:, :H], inv11)
    n12 = dot(inv11, v12)
    l22t, w22, x22 = block(g22 - dot(l21, l21t), t[H:, H:] - dot(k21, v12))
    t21 = -dot(x22, dot(l21 + dot(l22t.T, k21), w11))
    unroot = 1.0 / root
    lt_ref[:H, :H] = l11t * unroot
    lt_ref[:H, H:] = l21t * unroot
    lt_ref[H:, :H] = jnp.zeros((H, H), jnp.float32)
    lt_ref[H:, H:] = l22t * unroot
    tt_ref[:H, :H] = (x11 - dot(n12, t21)) * scale
    tt_ref[:H, H:] = -dot(n12, x22) * scale
    tt_ref[H:, :H] = t21 * scale
    tt_ref[H:, H:] = x22 * scale


def factor(pieces):
    vmem = pl.BlockSpec(memory_space=pltpu.VMEM)
    square = pltpu.VMEM((H, H), jnp.float32)
    return pl.pallas_call(
        factor_kernel,
        out_shape=[jax.ShapeDtypeStruct((W, W), jnp.float32)] * 2,
        in_specs=[vmem],
        out_specs=[vmem] * 2,
        compiler_params=pltpu.CompilerParams(vmem_limit_bytes=8 * 1024 * 1024),
        scratch_shapes=[square] * 4 + [pltpu.VMEM((PANEL, PANEL + 2, H), jnp.float32), pltpu.VMEM((W, 2 * W), jnp.float32)],
        cost_estimate=pl.CostEstimate(flops=2 * W**3, bytes_accessed=16 * W * W, transcendentals=0),
    )(pieces)


def to_tiles(x):
    rows, cols = x.shape
    return x.reshape(rows // 8, 8, cols // H, H).transpose(0, 2, 1, 3).reshape(rows * cols // (8 * H), 8, H)


def from_tiles(x, rows, cols):
    return x.reshape(rows // 8, cols // H, 8, H).transpose(0, 2, 1, 3).reshape(rows, cols)


def split(x):
    high = x.astype(jnp.bfloat16)
    return high, (x - high.astype(jnp.float32)).astype(jnp.bfloat16)


NN = ((1,), (0,))
NT = ((1,), (1,))
VMEM_BYTES = 60 * 1024 * 1024
TILE = 512
EARLY = 1


def dots(a, b, contract):
    a_high, a_low = split(a)
    b_high, b_low = split(b)
    left = jnp.concatenate([a_high, a_high, a_low], axis=contract[0][0])
    right = jnp.concatenate([b_high, b_low, b_high], axis=contract[1][0])
    return lax.dot_general(left, right, (contract, ((), ())), preferred_element_type=jnp.float32)


def product_kernel(place_ref, a_ref, cols_ref, rows_ref, lt_ref, keep_ref, send_ref, acc, inner_scr):
    step = pl.program_id(0)
    steps = pl.num_programs(0)

    @pl.when(step == 0)
    def _():
        own = (place_ref[1] == 0).astype(jnp.float32)
        cols = cols_ref[0]
        cols = jnp.concatenate([cols[:, :W] + own * lt_ref[...].T, cols[:, W:]], axis=1)
        acc[...] = dots(a_ref[...], cols, NT)

    @pl.when(step > 0)
    def _():
        acc[...] += dots(a_ref[...], cols_ref[0], NT)

    @pl.when(step == steps - 1)
    def _():
        own = (place_ref[0] == 0).astype(jnp.float32)
        inner = dots(rows_ref[:, :W] + own * lt_ref[...].T, acc[:W], NN)
        inner = inner + dots(rows_ref[:, W:], acc[W:], NN)
        inner_scr[...] = inner
        lines = keep_ref.shape[0]
        part = acc.shape[0] // (2 * lines)
        size = W // (2 * lines)
        line = place_ref[1] // 2
        core = place_ref[1] % 2
        for q in range(lines):
            for target, k in ((keep_ref, core), (send_ref, 1 - core)):
                i = 2 * ((line + q) % lines) + k
                target[q, :part] = acc[pl.ds(pl.multiple_of(i * part, 8), part)]
                target[q, part:] = inner_scr[pl.ds(pl.multiple_of(i * size, 8), size)]


def product(place, trailing, panel_cols, panel_rows, factor_t, parts):
    rows, cols = trailing.shape
    half = panel_cols.shape[2]
    tile = 640
    per = half // tile
    out = jax.ShapeDtypeStruct((parts // 2, (rows + W) // parts, W), jnp.float32)
    out_spec = pl.BlockSpec(out.shape, lambda i: (0, 0, 0))
    return pl.pallas_call(
        product_kernel,
        grid=(cols // tile,),
        out_shape=[out, out],
        in_specs=[
            pl.BlockSpec(memory_space=pltpu.SMEM),
            pl.BlockSpec((rows, tile), lambda i: (0, i)),
            pl.BlockSpec((1, W, tile), lambda i: (i // per, 0, i % per)),
            pl.BlockSpec((W, rows), lambda i: (0, 0)),
            pl.BlockSpec((W, W), lambda i: (0, 0)),
        ],
        out_specs=[out_spec, out_spec],
        scratch_shapes=[pltpu.VMEM((rows, W), jnp.float32), pltpu.VMEM((W, W), jnp.float32)],
        compiler_params=pltpu.CompilerParams(vmem_limit_bytes=VMEM_BYTES),
        cost_estimate=pl.CostEstimate(flops=6 * rows * cols * W, bytes_accessed=4 * rows * cols, transcendentals=0),
    )(place, trailing, panel_cols, panel_rows, factor_t)


def parts_kernel(place_ref, cols_ref, rows_ref, lt_ref, left_ref, right_ref):
    half = cols_ref.shape[2]
    lt = lt_ref[...]
    for i in range(rows_ref.shape[1] // W):
        at = slice(i * W, (i + 1) * W)
        rows = rows_ref[:, at].T
        if i == 0:
            rows = rows + lt * (place_ref[0] == 0).astype(jnp.float32)
        high, low = split(rows)
        for p, part in enumerate((high, high, low)):
            left_ref[at, p * W : (p + 1) * W] = part
    for h in range(cols_ref.shape[0]):
        for i in range(half // W):
            cols = cols_ref[h, :, i * W : (i + 1) * W]
            if h == 0 and i == 0:
                cols = cols + lt.T * (place_ref[1] == 0).astype(jnp.float32)
            high, low = split(cols)
            at = slice(h * half + i * W, h * half + (i + 1) * W)
            for p, part in enumerate((high, low, high)):
                right_ref[p * W : (p + 1) * W, at] = part


def parts_of(place, panel_cols, panel_rows, factor_t):
    rows = panel_rows.shape[1]
    cols = panel_cols.shape[0] * panel_cols.shape[2]
    vmem = pl.BlockSpec(memory_space=pltpu.VMEM)
    return pl.pallas_call(
        parts_kernel,
        out_shape=[jax.ShapeDtypeStruct(shape, jnp.bfloat16) for shape in ((rows, 3 * W), (3 * W, cols))],
        in_specs=[pl.BlockSpec(memory_space=pltpu.SMEM)] + [vmem] * 3,
        out_specs=[vmem] * 2,
        compiler_params=pltpu.CompilerParams(vmem_limit_bytes=VMEM_BYTES),
        cost_estimate=pl.CostEstimate(flops=8 * rows * W, bytes_accessed=10 * (rows + cols) * W, transcendentals=0),
    )(place, panel_cols, panel_rows, factor_t)


def correct_kernel(place_ref, left_ref, own_ref, other_ref, tt_ref, inner_ref, out_ref):
    t = tt_ref[...]
    mid = jnp.dot(t, inner_ref[...], precision=HIGHEST, preferred_element_type=jnp.float32)
    square = lax.dot_general(mid, t, (NT, ((), ())), precision=HIGHEST, preferred_element_type=jnp.float32)
    high, low = split(square)
    right = jnp.concatenate([high, low, high], axis=0)
    core = place_ref[1] % 2
    line = place_ref[1] // 2
    lines, part = own_ref.shape[:2]
    for s in range(lines):
        before = (line + lines - s) % lines
        for ref, k in ((own_ref, core), (other_ref, 1 - core)):
            at = pl.multiple_of((2 * before + k) * part, 16)
            weights = ref[s] - jnp.dot(left_ref[pl.ds(at, part)], right, preferred_element_type=jnp.float32)
            high, low = split(weights)
            out_ref[pl.ds(at, part)] = jnp.concatenate([high, high, low], axis=1)


def correct(place, left, own, other, coupling_t, inner):
    vmem = pl.BlockSpec(memory_space=pltpu.VMEM)
    return pl.pallas_call(
        correct_kernel,
        out_shape=jax.ShapeDtypeStruct(left.shape, jnp.bfloat16),
        in_specs=[pl.BlockSpec(memory_space=pltpu.SMEM)] + [vmem] * 5,
        out_specs=vmem,
        compiler_params=pltpu.CompilerParams(vmem_limit_bytes=VMEM_BYTES),
        cost_estimate=pl.CostEstimate(flops=2 * left.size * W, bytes_accessed=8 * left.size, transcendentals=0),
    )(place, left, own, other, coupling_t, inner)


def early_kernel(a_ref, left_ref, right_ref, out_ref):
    out_ref[...] = a_ref[...] - jnp.dot(left_ref[...], right_ref[...], preferred_element_type=jnp.float32)


def early(trailing, weight_left, right):
    rows = trailing.shape[0]
    return pl.pallas_call(
        early_kernel,
        grid=(EARLY,),
        out_shape=jax.ShapeDtypeStruct((rows, EARLY * TILE), jnp.float32),
        in_specs=[
            pl.BlockSpec((rows, TILE), lambda i: (0, i)),
            pl.BlockSpec((rows, 3 * W), lambda i: (0, 0)),
            pl.BlockSpec((3 * W, TILE), lambda i: (0, i)),
        ],
        out_specs=pl.BlockSpec((rows, TILE), lambda i: (0, i)),
        compiler_params=pltpu.CompilerParams(vmem_limit_bytes=VMEM_BYTES),
        cost_estimate=pl.CostEstimate(flops=6 * EARLY * TILE * rows * W, bytes_accessed=8 * EARLY * TILE * rows, transcendentals=0),
    )(trailing, weight_left, right)


def update_kernel(a_ref, early_ref, left_ref, wleft_ref, right_ref, weights_ref, out_ref, wleft, held, copies):
    step = pl.program_id(0)
    late = pl.num_programs(0) - EARLY
    second_left = pltpu.make_async_copy(wleft_ref, wleft, copies.at[EARLY])
    fetches = [
        pltpu.make_async_copy(early_ref.at[:, e * TILE : (e + 1) * TILE], held.at[e], copies.at[e]) for e in range(EARLY)
    ]

    @pl.when(step == 0)
    def _():
        second_left.start()
        for fetch in fetches:
            fetch.start()

    high, low = split(weights_ref[...].T)
    right = jnp.concatenate([high, low, high], axis=0)
    first = jnp.dot(left_ref[...], right, preferred_element_type=jnp.float32)

    @pl.when(step == 0)
    def _():
        second_left.wait()

    @pl.when(step < late)
    def _():
        second = jnp.dot(wleft[...], right_ref[...], preferred_element_type=jnp.float32)
        out_ref[...] = a_ref[...] - (first + second)

    for e in range(EARLY):

        @pl.when(step == late + e)
        def _(e=e):
            fetches[e].wait()
            out_ref[...] = held[e] - first


def update(trailing, early_cols, left, weight_left, right, weight_cols):
    rows, cols = trailing.shape
    steps = cols // TILE
    late = steps - EARLY
    anywhere = pl.BlockSpec(memory_space=pl.ANY)
    return pl.pallas_call(
        update_kernel,
        grid=(steps,),
        out_shape=jax.ShapeDtypeStruct((rows, cols), jnp.float32),
        in_specs=[
            pl.BlockSpec((rows, TILE), lambda i: (0, EARLY + jnp.minimum(i, late - 1))),
            anywhere,
            pl.BlockSpec((rows, 3 * W), lambda i: (0, 0)),
            anywhere,
            pl.BlockSpec((3 * W, TILE), lambda i: (0, EARLY + jnp.minimum(i, late - 1))),
            pl.BlockSpec((TILE, W), lambda i: ((i + EARLY) % steps, 0)),
        ],
        out_specs=pl.BlockSpec((rows, TILE), lambda i: (0, (i + EARLY) % steps)),
        scratch_shapes=[
            pltpu.VMEM((rows, 3 * W), jnp.bfloat16),
            pltpu.VMEM((EARLY, rows, TILE), jnp.float32),
            pltpu.SemaphoreType.DMA((EARLY + 1,)),
        ],
        compiler_params=pltpu.CompilerParams(vmem_limit_bytes=VMEM_BYTES),
        cost_estimate=pl.CostEstimate(flops=12 * rows * cols * W, bytes_accessed=8 * rows * cols, transcendentals=0),
    )(trailing, early_cols, left, weight_left, right, weight_cols)


def shards(trailing, panel_block):
    r = lax.axis_index("row")
    c = lax.axis_index("col")
    nr = lax.axis_size("row")
    nc = lax.axis_size("col")
    ratio = nr // nc
    perm = [(i * nc + j, ((i % ratio) * nc + j) * nc + i // ratio) for i in range(nr) for j in range(nc)]
    pair = [(j, j ^ 1) for j in range(nc)]
    lines = [list(range(k, nc, 2)) for k in range(2)]
    place = jnp.stack([r, c]).astype(jnp.int32)
    rows, width = panel_block.shape
    part = rows // nc
    panel_t = panel_block.T
    moved = lax.ppermute(panel_t, BOTH, perm)
    line = lax.all_gather(panel_t, "col", axis=0, axis_index_groups=lines)
    line, moved = lax.optimization_barrier((line, moved))
    other = lax.ppermute(line, "col", pair)
    even = c % 2 == 0
    panel_rows = jnp.stack([jnp.where(even, line, other), jnp.where(even, other, line)], axis=1).reshape(W, rows)
    panel_cols = lax.all_gather(moved, "row", axis=0, tiled=True).reshape(ratio, W, rows)
    strip = lax.dot_general(panel_t, panel_rows, (((1,), (1,)), ((), ())), precision=HIGHEST)
    top = jnp.where(r == 0, panel_t[:, :W], jnp.zeros((width, W), jnp.float32))
    pieces = to_tiles(jnp.concatenate([strip, top], axis=1))
    mine = jnp.sum(lax.all_to_all(pieces, "row", 0, 0, tiled=True), axis=0)
    full = lax.all_to_all(jnp.broadcast_to(mine[None], (nr * nc,) + mine.shape), BOTH, 0, 0, tiled=True)
    factor_t, coupling_t = factor(full)
    keep, send = product(place, trailing, panel_cols, panel_rows, factor_t, nc)
    pieces = keep + lax.ppermute(send, "col", pair)
    shifts = [[(j, (j + 2 * s) % nc) for j in range(nc)] for s in range(1, nc // 2)]
    pieces = pieces[0] + sum(lax.ppermute(pieces[s + 1], "col", shift) for s, shift in enumerate(shifts))
    mine, inner = pieces[:part], pieces[part:]
    mine = lax.dot_general(mine, coupling_t, (((1,), (1,)), ((), ())), precision=HIGHEST)
    mine, later = lax.optimization_barrier((mine, panel_rows))
    moved = lax.ppermute(mine, BOTH, perm)
    left, right = parts_of(place, panel_cols, later, factor_t)
    moved, left = lax.optimization_barrier((moved, left))
    weight_cols = lax.all_gather(moved, "row", axis=0, tiled=True)
    line = jnp.stack([mine] + [lax.ppermute(mine, "col", shift) for shift in shifts])
    half = (nr, 8 * W * W // (8 * H * nr * nc), H)
    inner = jnp.sum(lax.all_to_all(to_tiles(inner).reshape(half), "row", 0, 0, tiled=True), axis=0)
    line, inner = lax.optimization_barrier((line, inner))
    other = lax.ppermute(line, "col", pair)
    inner = jnp.broadcast_to(inner[None], (nr * nc,) + inner.shape)
    inner = lax.all_to_all(inner, BOTH, 0, 0, tiled=True).reshape((nr, nc) + inner.shape[1:])
    inner = from_tiles(inner.transpose(1, 0, 2, 3).reshape(-1, 8, H), W, W)
    weight_left = correct(place, left, line, other, coupling_t, inner)
    early_cols = early(trailing, weight_left, right)
    return update(trailing, early_cols, left, weight_left, right, weight_cols)


def solution(mesh):
    return jax.shard_map(shards, mesh=mesh, in_specs=(P("row", "col"), P("row", "col")), out_specs=P("row", "col"), check_vma=False)
```

```python
import jax
import jax.numpy as jnp
from jax import lax
from jax.experimental import pallas as pl
from jax.experimental.pallas import tpu as pltpu
from jax.sharding import PartitionSpec as P

W = 256
H = 128
PANEL = 8
STRIPS = 8
BOTH = ("row", "col")
HIGHEST = lax.Precision.HIGHEST


def lane(x, l):
    if x.shape[0] == 1:
        return lane(jnp.broadcast_to(x, (8, H)), l)[0:1]
    return jnp.take_along_axis(x, jnp.full(x.shape, l, jnp.int32), axis=1, mode="promise_in_bounds")


def panel_step(solo, rows, at):
    li = lax.broadcasted_iota(jnp.int32, (1, H), 1)
    sub = lax.broadcasted_iota(jnp.int32, (PANEL, H), 0)
    cols = [lane(rows, at + k) for k in range(PANEL)]
    mods, ratios, marks = [], [], []
    for a in range(PANEL):
        here = li == at + a
        row = rows[a : a + 1]
        tops = [cols[k][a : a + 1] for k in range(PANEL)]
        mod, ratio, final, mark = solo(a, here, row, tops)
        mods.append(mod)
        ratios.append(ratio)
        marks.append(mark)
        own = sub == a
        rows = jnp.where(own, final, rows - cols[a] * mod)
        for k in range(a + 1, PANEL):
            cols[k] = jnp.where(own, ratio[k], cols[k] - cols[a] * ratio[k])
    for a in range(PANEL - 2, -1, -1):
        for k in range(a + 1, PANEL):
            mods[a] = mods[a] - ratios[a][k] * mods[k]
    return rows, mods, marks


def update_rows(mat, first, cols, mods):
    new = mat[first:]
    for col, mod in zip(cols, mods):
        new = new - col * mod
    mat[first:] = new


def factor_kernel(pieces_ref, lt_ref, tt_ref, gw, vr, lt, lw, spread, whole):
    ri = lax.broadcasted_iota(jnp.int32, (W, W), 0)
    ci = lax.broadcasted_iota(jnp.int32, (W, W), 1)
    li = lax.broadcasted_iota(jnp.int32, (1, H), 1)
    across = 2 * W // H
    strip = W // STRIPS
    tiles = strip // 8 * across
    for t in range(tiles):
        for c in range(STRIPS):
            row = c * strip + t // across * 8
            whole[row : row + 8, t % across * H : (t % across + 1) * H] = pieces_ref[t * STRIPS + c]
    g = whole[:, :W]
    scale = 1.0 / jnp.max(jnp.where(ri == ci, g, 0.0), keepdims=True)
    root = jnp.sqrt(scale)
    t = whole[:, W:].T * root
    g = g * scale

    def dot(x, y):
        return jnp.dot(x, y, precision=HIGHEST, preferred_element_type=jnp.float32)

    def chol_panel(at):
        old = [lane(gw[at:], at + k) for k in range(PANEL)]

        def solo(a, here, row, tops):
            d = tops[a]
            inv = 1.0 / d
            rs = lax.rsqrt(d)
            rs = rs * (1.5 - 0.5 * d * rs * rs)
            scaled = row * rs
            mod = jnp.where(here, 1.0 + inv, row * inv)
            ratio = [top * inv for top in tops]
            upper = jnp.where(li >= at + a, scaled, 0.0)
            lower = jnp.where(here, rs, jnp.where(li < at + a, scaled, 0.0))
            marks = [rs, scaled] + [top * rs for top in tops]
            return mod, ratio, row, (upper, lower, marks)

        _, mods, marks = panel_step(solo, gw[pl.ds(at, PANEL), :], at)
        update_rows(gw, at, old, mods)
        lt[pl.ds(at, PANEL), :] = jnp.concatenate([m[0] for m in marks], axis=0)
        lw[pl.ds(at, PANEL), :] = jnp.concatenate([m[1] for m in marks], axis=0)
        for a in range(PANEL):
            for i, x in enumerate(marks[a][2]):
                if i < 2 or i - 2 >= a:
                    spread[a, i : i + 1, :] = x

    def jordan_panel(at):
        old = [lane(vr[...], at + k) for k in range(PANEL)]
        marks = [[spread[a, i : i + 1, :] for i in range(PANEL + 2)] for a in range(PANEL)]

        def solo(a, here, row, tops):
            rs, scaled = marks[a][:2]
            row = row + scaled
            q = 1.0 / (tops[a] + marks[a][2 + a])
            norm = row * q
            rq = rs * q
            mod = jnp.where(here, 1.0 + rq, norm)
            final = jnp.where(here, rq, norm)
            ratio = [(tops[k] + marks[a][2 + k]) * q if k > a else None for k in range(PANEL)]
            return mod, ratio, final, None

        rows, mods, _ = panel_step(solo, vr[pl.ds(at, PANEL), :], at)
        update_rows(vr, 0, old, mods)
        vr[pl.ds(at, PANEL), :] = rows

    def block(gram, top):
        gw[...] = gram
        vr[...] = top
        chol_panel(0)
        for at in range(PANEL, H, PANEL):
            jordan_panel(at - PANEL)
            chol_panel(at)
        jordan_panel(H - PANEL)
        return lt[...], lw[...], vr[...]

    g12, g22 = g[:H, H:], g[H:, H:]
    l11t, w11, x11 = block(g[:H, :H], t[:H, :H])
    l21t = dot(w11, g12)
    l21 = l21t.T
    inv11 = dot(x11, l11t.T)
    v12 = t[:H, H:] + l21t
    k21 = dot(t[H:, :H], inv11)
    n12 = dot(inv11, v12)
    l22t, w22, x22 = block(g22 - dot(l21, l21t), t[H:, H:] - dot(k21, v12))
    t21 = -dot(x22, dot(l21 + dot(l22t.T, k21), w11))
    unroot = 1.0 / root
    lt_ref[:H, :H] = l11t * unroot
    lt_ref[:H, H:] = l21t * unroot
    lt_ref[H:, :H] = jnp.zeros((H, H), jnp.float32)
    lt_ref[H:, H:] = l22t * unroot
    tt_ref[:H, :H] = (x11 - dot(n12, t21)) * scale
    tt_ref[:H, H:] = -dot(n12, x22) * scale
    tt_ref[H:, :H] = t21 * scale
    tt_ref[H:, H:] = x22 * scale


def factor(pieces):
    vmem = pl.BlockSpec(memory_space=pltpu.VMEM)
    square = pltpu.VMEM((H, H), jnp.float32)
    return pl.pallas_call(
        factor_kernel,
        out_shape=[jax.ShapeDtypeStruct((W, W), jnp.float32)] * 2,
        in_specs=[vmem],
        out_specs=[vmem] * 2,
        compiler_params=pltpu.CompilerParams(vmem_limit_bytes=8 * 1024 * 1024),
        scratch_shapes=[square] * 4 + [pltpu.VMEM((PANEL, PANEL + 2, H), jnp.float32), pltpu.VMEM((W, 2 * W), jnp.float32)],
        cost_estimate=pl.CostEstimate(flops=2 * W**3, bytes_accessed=16 * W * W, transcendentals=0),
    )(pieces)


def to_tiles(x):
    rows, cols = x.shape
    return x.reshape(rows // 8, 8, cols // H, H).transpose(0, 2, 1, 3).reshape(rows * cols // (8 * H), 8, H)


def from_tiles(x, rows, cols):
    return x.reshape(rows // 8, cols // H, 8, H).transpose(0, 2, 1, 3).reshape(rows, cols)


def split(x):
    high = x.astype(jnp.bfloat16)
    return high, (x - high.astype(jnp.float32)).astype(jnp.bfloat16)


NN = ((1,), (0,))
NT = ((1,), (1,))
VMEM_BYTES = 60 * 1024 * 1024
TILE = 512
EARLY = 1


def dots(a, b, contract):
    a_high, a_low = split(a)
    b_high, b_low = split(b)
    left = jnp.concatenate([a_high, a_high, a_low], axis=contract[0][0])
    right = jnp.concatenate([b_high, b_low, b_high], axis=contract[1][0])
    return lax.dot_general(left, right, (contract, ((), ())), preferred_element_type=jnp.float32)


def product_kernel(place_ref, a_ref, cols_ref, rows_ref, lt_ref, keep_ref, send_ref, acc, inner_scr, panel, arrived):
    step = pl.program_id(0)
    steps = pl.num_programs(0)
    fetch = pltpu.make_async_copy(rows_ref, panel, arrived)

    @pl.when(step == 0)
    def _():
        fetch.start()
        own = (place_ref[1] == 0).astype(jnp.float32)
        cols = cols_ref[0]
        cols = jnp.concatenate([cols[:, :W] + own * lt_ref[...].T, cols[:, W:]], axis=1)
        acc[...] = dots(a_ref[...], cols, NT)

    @pl.when(step > 0)
    def _():
        acc[...] += dots(a_ref[...], cols_ref[0], NT)

    @pl.when(step == steps - 1)
    def _():
        fetch.wait()
        own = (place_ref[0] == 0).astype(jnp.float32)
        inner = dots(panel[:, :W] + own * lt_ref[...].T, acc[:W], NN)
        inner = inner + dots(panel[:, W:], acc[W:], NN)
        inner_scr[...] = inner
        lines = keep_ref.shape[0]
        part = acc.shape[0] // (2 * lines)
        size = W // (2 * lines)
        line = place_ref[1] // 2
        core = place_ref[1] % 2
        for q in range(lines):
            for target, k in ((keep_ref, core), (send_ref, 1 - core)):
                i = 2 * ((line + q) % lines) + k
                target[q, :part] = acc[pl.ds(pl.multiple_of(i * part, 8), part)]
                target[q, part:] = inner_scr[pl.ds(pl.multiple_of(i * size, 8), size)]


def product(place, trailing, panel_cols, panel_rows, factor_t, parts):
    rows, cols = trailing.shape
    half = panel_cols.shape[2]
    tile = 640
    per = half // tile
    out = jax.ShapeDtypeStruct((parts // 2, (rows + W) // parts, W), jnp.float32)
    out_spec = pl.BlockSpec(out.shape, lambda i: (0, 0, 0))
    return pl.pallas_call(
        product_kernel,
        grid=(cols // tile,),
        out_shape=[out, out],
        in_specs=[
            pl.BlockSpec(memory_space=pltpu.SMEM),
            pl.BlockSpec((rows, tile), lambda i: (0, i)),
            pl.BlockSpec((1, W, tile), lambda i: (i // per, 0, i % per)),
            pl.BlockSpec(memory_space=pl.ANY),
            pl.BlockSpec((W, W), lambda i: (0, 0)),
        ],
        out_specs=[out_spec, out_spec],
        scratch_shapes=[
            pltpu.VMEM((rows, W), jnp.float32),
            pltpu.VMEM((W, W), jnp.float32),
            pltpu.VMEM((W, rows), jnp.float32),
            pltpu.SemaphoreType.DMA,
        ],
        compiler_params=pltpu.CompilerParams(vmem_limit_bytes=VMEM_BYTES),
        cost_estimate=pl.CostEstimate(flops=6 * rows * cols * W, bytes_accessed=4 * rows * cols, transcendentals=0),
    )(place, trailing, panel_cols, panel_rows, factor_t)


def parts_kernel(place_ref, cols_ref, rows_ref, lt_ref, left_ref, right_ref):
    half = cols_ref.shape[2]
    lt = lt_ref[...]
    for i in range(rows_ref.shape[1] // W):
        at = slice(i * W, (i + 1) * W)
        rows = rows_ref[:, at].T
        if i == 0:
            rows = rows + lt * (place_ref[0] == 0).astype(jnp.float32)
        high, low = split(rows)
        for p, part in enumerate((high, high, low)):
            left_ref[at, p * W : (p + 1) * W] = part
    for h in range(cols_ref.shape[0]):
        for i in range(half // W):
            cols = cols_ref[h, :, i * W : (i + 1) * W]
            if h == 0 and i == 0:
                cols = cols + lt.T * (place_ref[1] == 0).astype(jnp.float32)
            high, low = split(cols)
            at = slice(h * half + i * W, h * half + (i + 1) * W)
            right_ref[:W, at] = high
            right_ref[W:, at] = low


def parts_of(place, panel_cols, panel_rows, factor_t):
    rows = panel_rows.shape[1]
    cols = panel_cols.shape[0] * panel_cols.shape[2]
    vmem = pl.BlockSpec(memory_space=pltpu.VMEM)
    return pl.pallas_call(
        parts_kernel,
        out_shape=[jax.ShapeDtypeStruct(shape, jnp.bfloat16) for shape in ((rows, 3 * W), (2 * W, cols))],
        in_specs=[pl.BlockSpec(memory_space=pltpu.SMEM)] + [vmem] * 3,
        out_specs=[vmem] * 2,
        compiler_params=pltpu.CompilerParams(vmem_limit_bytes=VMEM_BYTES),
        cost_estimate=pl.CostEstimate(flops=8 * rows * W, bytes_accessed=10 * (rows + cols) * W, transcendentals=0),
    )(place, panel_cols, panel_rows, factor_t)


def correct_kernel(place_ref, left_ref, own_ref, other_ref, tt_ref, inner_ref, out_ref):
    t = tt_ref[...]
    mid = jnp.dot(t, inner_ref[...], precision=HIGHEST, preferred_element_type=jnp.float32)
    square = lax.dot_general(mid, t, (NT, ((), ())), precision=HIGHEST, preferred_element_type=jnp.float32)
    high, low = split(square)
    right = jnp.concatenate([high, low, high], axis=0)
    core = place_ref[1] % 2
    line = place_ref[1] // 2
    lines, part = own_ref.shape[:2]
    for s in range(lines):
        before = (line + lines - s) % lines
        for ref, k in ((own_ref, core), (other_ref, 1 - core)):
            at = pl.multiple_of((2 * before + k) * part, 16)
            weights = ref[s] - jnp.dot(left_ref[pl.ds(at, part)], right, preferred_element_type=jnp.float32)
            high, low = split(weights)
            out_ref[pl.ds(at, part)] = jnp.concatenate([high, high, low], axis=1)


def correct(place, left, own, other, coupling_t, inner):
    vmem = pl.BlockSpec(memory_space=pltpu.VMEM)
    return pl.pallas_call(
        correct_kernel,
        out_shape=jax.ShapeDtypeStruct(left.shape, jnp.bfloat16),
        in_specs=[pl.BlockSpec(memory_space=pltpu.SMEM)] + [vmem] * 5,
        out_specs=vmem,
        compiler_params=pltpu.CompilerParams(vmem_limit_bytes=VMEM_BYTES),
        cost_estimate=pl.CostEstimate(flops=2 * left.size * W, bytes_accessed=8 * left.size, transcendentals=0),
    )(place, left, own, other, coupling_t, inner)


def stacked(ref):
    high = ref[:W]
    return jnp.concatenate([high, ref[W:], high], axis=0)


def early_kernel(a_ref, left_ref, right_ref, out_ref):
    out_ref[...] = a_ref[...] - jnp.dot(left_ref[...], stacked(right_ref), preferred_element_type=jnp.float32)


def early(trailing, weight_left, right):
    rows = trailing.shape[0]
    return pl.pallas_call(
        early_kernel,
        grid=(EARLY,),
        out_shape=jax.ShapeDtypeStruct((rows, EARLY * TILE), jnp.float32),
        in_specs=[
            pl.BlockSpec((rows, TILE), lambda i: (0, i)),
            pl.BlockSpec((rows, 3 * W), lambda i: (0, 0)),
            pl.BlockSpec((2 * W, TILE), lambda i: (0, i)),
        ],
        out_specs=pl.BlockSpec((rows, TILE), lambda i: (0, i)),
        compiler_params=pltpu.CompilerParams(vmem_limit_bytes=VMEM_BYTES),
        cost_estimate=pl.CostEstimate(flops=6 * EARLY * TILE * rows * W, bytes_accessed=8 * EARLY * TILE * rows, transcendentals=0),
    )(trailing, weight_left, right)


def update_kernel(a_ref, early_ref, left_ref, wleft_ref, right_ref, weights_ref, out_ref, wleft, held, copies):
    step = pl.program_id(0)
    late = pl.num_programs(0) - EARLY
    second_left = pltpu.make_async_copy(wleft_ref, wleft, copies.at[EARLY])
    fetches = [
        pltpu.make_async_copy(early_ref.at[:, e * TILE : (e + 1) * TILE], held.at[e], copies.at[e]) for e in range(EARLY)
    ]

    @pl.when(step == 0)
    def _():
        second_left.start()
        for fetch in fetches:
            fetch.start()

    high, low = split(weights_ref[...].T)
    right = jnp.concatenate([high, low, high], axis=0)
    first = jnp.dot(left_ref[...], right, preferred_element_type=jnp.float32)

    @pl.when(step == 0)
    def _():
        second_left.wait()

    @pl.when(step < late)
    def _():
        second = jnp.dot(wleft[...], stacked(right_ref), preferred_element_type=jnp.float32)
        out_ref[...] = a_ref[...] - (first + second)

    for e in range(EARLY):

        @pl.when(step == late + e)
        def _(e=e):
            fetches[e].wait()
            out_ref[...] = held[e] - first


def update(trailing, early_cols, left, weight_left, right, weight_cols):
    rows, cols = trailing.shape
    steps = cols // TILE
    late = steps - EARLY
    anywhere = pl.BlockSpec(memory_space=pl.ANY)
    return pl.pallas_call(
        update_kernel,
        grid=(steps,),
        out_shape=jax.ShapeDtypeStruct((rows, cols), jnp.float32),
        in_specs=[
            pl.BlockSpec((rows, TILE), lambda i: (0, EARLY + jnp.minimum(i, late - 1))),
            anywhere,
            pl.BlockSpec((rows, 3 * W), lambda i: (0, 0)),
            anywhere,
            pl.BlockSpec((2 * W, TILE), lambda i: (0, EARLY + jnp.minimum(i, late - 1))),
            pl.BlockSpec((TILE, W), lambda i: ((i + EARLY) % steps, 0)),
        ],
        out_specs=pl.BlockSpec((rows, TILE), lambda i: (0, (i + EARLY) % steps)),
        scratch_shapes=[
            pltpu.VMEM((rows, 3 * W), jnp.bfloat16),
            pltpu.VMEM((EARLY, rows, TILE), jnp.float32),
            pltpu.SemaphoreType.DMA((EARLY + 1,)),
        ],
        compiler_params=pltpu.CompilerParams(vmem_limit_bytes=VMEM_BYTES),
        cost_estimate=pl.CostEstimate(flops=12 * rows * cols * W, bytes_accessed=8 * rows * cols, transcendentals=0),
    )(trailing, early_cols, left, weight_left, right, weight_cols)


def shards(trailing, panel_block):
    r = lax.axis_index("row")
    c = lax.axis_index("col")
    nr = lax.axis_size("row")
    nc = lax.axis_size("col")
    ratio = nr // nc
    perm = [(i * nc + j, ((i % ratio) * nc + j) * nc + i // ratio) for i in range(nr) for j in range(nc)]
    pair = [(j, j ^ 1) for j in range(nc)]
    lines = [list(range(k, nc, 2)) for k in range(2)]
    place = jnp.stack([r, c]).astype(jnp.int32)
    rows, width = panel_block.shape
    part = rows // nc
    panel_t = panel_block.T
    moved = lax.ppermute(panel_t, BOTH, perm)
    line = lax.all_gather(panel_t, "col", axis=0, axis_index_groups=lines)
    line, moved = lax.optimization_barrier((line, moved))
    other = lax.ppermute(line, "col", pair)
    even = c % 2 == 0
    panel_rows = jnp.stack([jnp.where(even, line, other), jnp.where(even, other, line)], axis=1).reshape(W, rows)
    panel_cols = lax.all_gather(moved, "row", axis=0, tiled=True).reshape(ratio, W, rows)
    strip = lax.dot_general(panel_t, panel_rows, (((1,), (1,)), ((), ())), precision=HIGHEST)
    top = jnp.where(r == 0, panel_t[:, :W], jnp.zeros((width, W), jnp.float32))
    pieces = to_tiles(jnp.concatenate([strip, top], axis=1))
    mine = jnp.sum(lax.all_to_all(pieces, "row", 0, 0, tiled=True), axis=0)
    full = lax.all_to_all(jnp.broadcast_to(mine[None], (nr * nc,) + mine.shape), BOTH, 0, 0, tiled=True)
    factor_t, coupling_t = factor(full)
    keep, send = product(place, trailing, panel_cols, panel_rows, factor_t, nc)
    pieces = keep + lax.ppermute(send, "col", pair)
    shifts = [[(j, (j + 2 * s) % nc) for j in range(nc)] for s in range(1, nc // 2)]
    pieces = pieces[0] + sum(lax.ppermute(pieces[s + 1], "col", shift) for s, shift in enumerate(shifts))
    mine, inner = pieces[:part], pieces[part:]
    mine = lax.dot_general(mine, coupling_t, (((1,), (1,)), ((), ())), precision=HIGHEST)
    mine, later = lax.optimization_barrier((mine, panel_rows))
    moved = lax.ppermute(mine, BOTH, perm)
    left, right = parts_of(place, panel_cols, later, factor_t)
    moved, left = lax.optimization_barrier((moved, left))
    weight_cols = lax.all_gather(moved, "row", axis=0, tiled=True)
    line = jnp.stack([mine] + [lax.ppermute(mine, "col", shift) for shift in shifts])
    half = (nr, 8 * W * W // (8 * H * nr * nc), H)
    inner = jnp.sum(lax.all_to_all(to_tiles(inner).reshape(half), "row", 0, 0, tiled=True), axis=0)
    line, inner = lax.optimization_barrier((line, inner))
    other = lax.ppermute(line, "col", pair)
    inner = jnp.broadcast_to(inner[None], (nr * nc,) + inner.shape)
    inner = lax.all_to_all(inner, BOTH, 0, 0, tiled=True).reshape((nr, nc) + inner.shape[1:])
    inner = from_tiles(inner.transpose(1, 0, 2, 3).reshape(-1, 8, H), W, W)
    weight_left = correct(place, left, line, other, coupling_t, inner)
    early_cols = early(trailing, weight_left, right)
    return update(trailing, early_cols, left, weight_left, right, weight_cols)


def solution(mesh):
    return jax.shard_map(shards, mesh=mesh, in_specs=(P("row", "col"), P("row", "col")), out_specs=P("row", "col"), check_vma=False)
```
